256 devices in a mesh: dp: 4 (over x_lo, core), ctx: 8 (over z), head: 8 (over y, x_hi).
Axes of the slice: x: 4 (x_hi: 2, x_lo: 2; x = x_hi * 2 + x_lo), y: 4, z: 8, core: 2. Of those that a mesh axis runs over, the one named last changes fastest.
Arguments:
- query_matrix: bfloat16 [4, 2048, 8, 8, 128], P('dp', 'ctx', 'head'), may hold values from -180 to 180
- key_matrix: bfloat16 [4, 2048, 8, 128], P('dp', 'ctx', 'head'), may hold values from -6 to 6
- value_matrix: bfloat16 [4, 2048, 8, 128], P('dp', 'ctx', 'head'), may hold values from -6 to 6
- output_gradient: bfloat16 [4, 2048, 8, 8, 128], P('dp', 'ctx', 'head'), may hold values from -6 to 6
- normed_layer_input: bfloat16 [4, 2048, 8192], P('dp', 'ctx', 'head'), may hold values from -6 to 6
- adapter_down: bfloat16 [8192, 8], P('head'), may hold values from -0.0625 to 0.0625
- adapter_up: bfloat16 [8, 8, 8, 128], P(None, 'head'), may hold values from -2 to 2
- lengths: int32 [4], P('dp'), may hold values from 1024 to 2048, as said below
Outputs:
- query_gradient: bfloat16 [4, 2048, 8, 8, 128], P('dp', 'ctx', 'head')
- key_gradient: bfloat16 [4, 2048, 8, 128], P('dp', 'ctx', 'head')
- value_gradient: bfloat16 [4, 2048, 8, 128], P('dp', 'ctx', 'head')
- down_matrix_gradient: float32 [8192, 8], P('head')
- up_matrix_gradient: float32 [8, 8, 8, 128], P(None, 'head')
The draws below stay inside these ranges and needn't reach their ends.
Inputs may be any that keep to these rules, and one draw needn't show every extreme that they name: `lengths`: each value is at least half a sequence, and some sequence is whole.
All inputs are finite; a program needn't handle non-finite values.
Results may differ from the reference program's by a relative error of at most 0.014.
Values may be sent and summed in bfloat16 or wider, within the bound.
A program may use at most 64 MiB of HBM per device.

```python
import math
import jax
import jax.numpy as jnp
from jax import lax

MODEL_WIDTH = 8192
KEY_VALUE_HEADS = 8
HEAD_SIZE = 128
ADAPTER_RANK = 8
TOK_DEV = 256
QUERY_PER_GROUP = 8
SEQS = 4
SEQ = 2048


def base_keys(key):
    return jnp.clip(jax.random.normal(key, (SEQS, SEQ, KEY_VALUE_HEADS, HEAD_SIZE), jnp.float32), -6.0, 6.0)


def draw_key_matrix(key, part):
    base = base_keys(key)
    return base.astype(jnp.bfloat16)


def draw_query_matrix(key, part):
    key = jax.random.fold_in(key, 3)
    fresh = jnp.clip(jax.random.normal(key, (SEQS, SEQ, KEY_VALUE_HEADS, QUERY_PER_GROUP, HEAD_SIZE), jnp.float32), -6.0, 6.0)
    return fresh.astype(jnp.bfloat16)


def draw_lengths(key, part):
    key = jax.random.fold_in(key, 7)
    first, second = jax.random.split(key)
    drawn = jax.random.randint(first, (SEQS,), SEQ // 2, SEQ + 1)
    whole = jax.random.randint(second, (), 0, SEQS)
    return jnp.where(jnp.arange(SEQS, dtype=jnp.int32) == whole, SEQ, drawn).astype(jnp.int32)


def level_of(stream_key, dims, cuts, least, largest):
    loudness = 1.0
    for axis_at, shards_of in cuts:
        draws = jax.random.uniform(jax.random.fold_in(jax.random.fold_in(stream_key, 6), axis_at), (shards_of,), jnp.float32, least / len(cuts), largest / len(cuts))
        loudness = loudness * jnp.repeat(jnp.exp(draws), dims[axis_at] // shards_of).reshape((-1,) + (1,) * (len(dims) - 1 - axis_at))
    return loudness


def scatter_about(key, dims, scale, reach, shards=(), kind=jnp.bfloat16):
    values = jax.random.normal(key, dims, jnp.float32) * scale
    if len(shards) > 0:
        values = level_of(key, dims, shards, -0.22, 0.18) * values
    return jnp.clip(values, min=-reach, max=reach).astype(kind)


def setup_inputs(seed: int = 0) -> dict:
    key_of = jax.random.split(jax.random.key(seed), 9)
    return {
        "query_matrix": draw_query_matrix(jax.random.fold_in(key_of[8], 71), 0),
        "key_matrix": draw_key_matrix(jax.random.fold_in(key_of[8], 71), 0),
        "value_matrix": scatter_about(key_of[2], (SEQS, SEQ, KEY_VALUE_HEADS, HEAD_SIZE), 1.0, 6.0, ((0, 4), (1, 8), (2, 8))),
        "output_gradient": scatter_about(key_of[3], (SEQS, SEQ, KEY_VALUE_HEADS, QUERY_PER_GROUP, HEAD_SIZE), 1.0, 6.0, ((0, 4), (1, 8), (2, 8))),
        "normed_layer_input": scatter_about(key_of[4], (SEQS, SEQ, MODEL_WIDTH), 1.0, 6.0, ((0, 4), (1, 8), (2, 8))),
        "adapter_down": scatter_about(key_of[5], (MODEL_WIDTH, ADAPTER_RANK), MODEL_WIDTH ** -0.5, 0.0625, ((0, 8),)),
        "adapter_up": scatter_about(key_of[6], (ADAPTER_RANK, KEY_VALUE_HEADS, QUERY_PER_GROUP, HEAD_SIZE), ADAPTER_RANK ** -0.5, 2.0, ((1, 8),)),
        "lengths": draw_lengths(jax.random.fold_in(key_of[8], 71), 0),
    }


ADAPTER_SCALE = 2.0
BLOCKED = -1e+30

def group_backward(query_matrix, key_matrix, value_matrix, output_gradient, positions, length):
    softmax_scale = 1.0 / math.sqrt(query_matrix.shape[-1])
    count = query_matrix.shape[0]
    index = jnp.arange(count, dtype=jnp.int32)
    live = jnp.where((positions < length)[:, None, None], output_gradient, jnp.zeros_like(output_gradient))
    queries_wide = query_matrix.astype(jnp.float32)
    keys_wide = key_matrix.astype(jnp.float32)
    values_wide = value_matrix.astype(jnp.float32)
    live_wide = live.astype(jnp.float32)
    scores = jnp.einsum('igd,jd->gij', queries_wide, keys_wide) * softmax_scale
    allowed = (index[None, :] <= index[:, None]) & ((positions < length)[None, :] | (index[None, :] == index[:, None]))
    scores = jnp.where(allowed[None], scores, BLOCKED)
    row_max = lax.optimization_barrier(jnp.max(scores, axis=-1, keepdims=True))
    weights = jnp.exp(scores - row_max)
    probs = weights / lax.optimization_barrier(jnp.sum(weights, axis=-1, keepdims=True))
    probs_low = probs.astype(jnp.bfloat16).astype(jnp.float32)
    output = jnp.einsum('gij,jd->igd', probs_low, values_wide)
    out_dot = lax.optimization_barrier(jnp.sum(live_wide * output, axis=-1))
    prob_grad = jnp.einsum('igd,jd->gij', live_wide, values_wide)
    score_grad = (probs * (prob_grad - jnp.transpose(out_dot)[:, :, None])).astype(jnp.bfloat16).astype(jnp.float32)
    grad_q = (jnp.einsum('gij,jd->igd', score_grad, keys_wide) * softmax_scale).astype(jnp.bfloat16)
    grad_k = (jnp.einsum('gij,igd->jd', score_grad, queries_wide) * softmax_scale).astype(jnp.bfloat16)
    grad_v = jnp.einsum('gij,igd->jd', probs_low, live_wide).astype(jnp.bfloat16)
    return (grad_q, grad_k, grad_v)

def reference(query_matrix, key_matrix, value_matrix, output_gradient, normed_layer_input, adapter_down, adapter_up, lengths):
    seqs, seq_len, kv_heads, per_kv, width = query_matrix.shape
    group_rows = TOK_DEV
    half_rows = group_rows // 2
    groups = seq_len // group_rows
    positions = jnp.arange(seq_len, dtype=jnp.int32)

    def per_head(item):
        queries, keys_head, values_head, grads_head, length, offset = item

        def regroup(arr):
            rolled = jnp.roll(arr, -offset, axis=0)
            return rolled.reshape((groups, group_rows) + arr.shape[1:])

        def one_group(pieces):
            return group_backward(pieces[0], pieces[1], pieces[2], pieces[3], pieces[4], length)
        outs = lax.map(one_group, (regroup(queries), regroup(keys_head), regroup(values_head), regroup(grads_head), regroup(positions)))

        def unroll(arr):
            return jnp.roll(arr.reshape((seq_len,) + arr.shape[2:]), offset, axis=0)
        return (unroll(outs[0]), unroll(outs[1]), unroll(outs[2]))

    def flatten_heads(arr):
        moved = jnp.moveaxis(arr, 2, 1)
        return moved.reshape((seqs * kv_heads,) + moved.shape[2:])
    head_ids = jnp.tile(jnp.arange(kv_heads, dtype=jnp.int32), seqs)
    offsets = jnp.where(head_ids < kv_heads // 2, half_rows, 0).astype(jnp.int32)
    lengths_rep = jnp.repeat(lengths, kv_heads)
    grads = lax.map(per_head, (flatten_heads(query_matrix), flatten_heads(key_matrix), flatten_heads(value_matrix), flatten_heads(output_gradient), lengths_rep, offsets))

    def restore(arr):
        shaped = arr.reshape((seqs, kv_heads) + arr.shape[1:])
        return jnp.moveaxis(shaped, 1, 2)
    query_gradient = restore(grads[0])
    key_gradient = restore(grads[1])
    value_gradient = restore(grads[2])
    flattened_input = normed_layer_input.reshape(seqs * seq_len, -1)
    flattened_gradient = query_gradient.reshape(seqs * seq_len, -1)
    flattened_up = adapter_up.reshape(adapter_up.shape[0], -1)
    low_rank_input = jnp.dot(flattened_input, adapter_down, preferred_element_type=jnp.float32).astype(jnp.bfloat16)
    low_rank_gradient = lax.dot_general(flattened_gradient, flattened_up, (((1,), (1,)), ((), ())), preferred_element_type=jnp.float32).astype(jnp.bfloat16)
    up_matrix_gradient = ADAPTER_SCALE * lax.dot_general(low_rank_input, flattened_gradient, (((0,), (0,)), ((), ())), preferred_element_type=jnp.float32)
    down_matrix_gradient = ADAPTER_SCALE * lax.dot_general(flattened_input, low_rank_gradient, (((0,), (0,)), ((), ())), preferred_element_type=jnp.float32)
    return (query_gradient, key_gradient, value_gradient, down_matrix_gradient, up_matrix_gradient.reshape(adapter_up.shape))
```

```python
import functools
import math

import jax
import jax.numpy as jnp
from jax import lax
from jax.experimental import pallas as pl
from jax.experimental.pallas import tpu as pltpu
from jax.sharding import PartitionSpec as P

ADAPTER_SCALE = 2.0
BLOCKED = -1e30
MESH = pl.DeviceIdType.MESH
F32 = jnp.float32
BF16 = jnp.bfloat16
NT = (((1,), (1,)), ((), ()))
NN = (((1,), (0,)), ((), ()))
TN = (((0,), (0,)), ((), ()))


def mm(a, b, dims):
    return lax.dot_general(a, b, dims, preferred_element_type=F32)


def kernel(
    dims,
    q_in, k_in, v_in, do_in, x_in, at_in, u_in, len_in,
    dq_out, dk_out, dv_out, down_out, up_out,
    q_s, do_s, x_s, at_s, u_s, k_s, v_s,
    dq32, dq16, dqcat, dkv_out,
    acc_ke, acc_ve, acc_kl, acc_vl, ret_send, ret_recv,
    ri_buf, rg_buf, up_part, up_recv, up_all, dn_part, dn_recv, dn_all,
    load_sem, out_sem, kv_send, kv_recv, ret_sems, ri_sems, rg_sems,
    up_sems, upg_sems, dn_sems, dng_sems,
):
    nd, nc, nh, half, group, rank = dims
    rows = 2 * half
    hq = half * group
    here_d, here_c, here_h = lax.axis_index("dp"), lax.axis_index("ctx"), lax.axis_index("head")
    shifted = jnp.where(here_h < nh // 2, 1, 0)
    is_shifted = here_h < nh // 2
    early = shifted * half
    late = (1 - shifted) * half
    early_q = pl.multiple_of(shifted * hq, hq)
    late_q = pl.multiple_of((1 - shifted) * hq, hq)
    early_m = pl.multiple_of(early, half)
    late_m = pl.multiple_of(late, half)
    group_count = nd * nc
    me = here_d * nc + here_c
    after_c = lax.rem(here_c + 1, nc)
    before_c = lax.rem(here_c + nc - 1, nc)

    def local(src, dst, sem):
        return pltpu.make_async_copy(src, dst, sem)

    loads = [
        local(x_in, x_s, load_sem.at[0]),
        local(at_in, at_s, load_sem.at[1]),
        local(k_in.at[pl.ds(early_m, half)], k_s.at[pl.ds(0, half)], load_sem.at[2]),
        local(v_in.at[pl.ds(early_m, half)], v_s.at[pl.ds(0, half)], load_sem.at[3]),
        local(q_in.at[pl.ds(early_q, hq)], q_s.at[pl.ds(0, hq)], load_sem.at[4]),
        local(do_in.at[pl.ds(early_q, hq)], do_s.at[pl.ds(0, hq)], load_sem.at[5]),
        local(k_in.at[pl.ds(late_m, half)], k_s.at[pl.ds(rows, half)], load_sem.at[6]),
        local(v_in.at[pl.ds(late_m, half)], v_s.at[pl.ds(rows, half)], load_sem.at[7]),
        local(q_in.at[pl.ds(late_q, hq)], q_s.at[pl.ds(hq, hq)], load_sem.at[8]),
        local(do_in.at[pl.ds(late_q, hq)], do_s.at[pl.ds(hq, hq)], load_sem.at[9]),
        local(u_in, u_s, load_sem.at[10]),
    ]
    for load in loads:
        load.start()

    barrier = pltpu.get_barrier_semaphore()

    def greet_group(step, carry):
        peer = lax.rem(me + step, group_count)
        pl.semaphore_signal(
            barrier, inc=1, device_id=(peer // nc, lax.rem(peer, nc), here_h), device_id_type=MESH
        )
        return carry

    def greet_head(step, carry):
        pl.semaphore_signal(
            barrier, inc=1, device_id=(here_d, here_c, lax.rem(here_h + step, nh)), device_id_type=MESH
        )
        return carry

    lax.fori_loop(1, group_count, greet_group, 0)
    lax.fori_loop(1, nh, greet_head, 0)

    loads[0].wait()
    loads[1].wait()
    ri_buf[here_h] = mm(at_s[...], x_s[...], NT)

    pl.semaphore_wait(barrier, group_count - 1 + nh - 1)
    loads[2].wait()
    loads[3].wait()

    def kv_copy(ref, at):
        return pltpu.make_async_remote_copy(
            src_ref=ref.at[pl.ds(0, half)],
            dst_ref=ref.at[pl.ds(half, half)],
            send_sem=kv_send.at[at],
            recv_sem=kv_recv.at[at],
            device_id=(here_d, after_c, here_h),
            device_id_type=MESH,
        )

    @pl.when(is_shifted)
    def _():
        kv_copy(k_s, 0).start()
        kv_copy(v_s, 1).start()

    @pl.when(jnp.logical_not(is_shifted))
    def _():
        k_s[half:rows] = k_s[0:half]
        v_s[half:rows] = v_s[0:half]

    def head_exchange(buf, sems):
        def send(step, carry):
            peer = lax.rem(here_h + step, nh)
            pltpu.make_async_remote_copy(
                src_ref=buf.at[here_h],
                dst_ref=buf.at[here_h],
                send_sem=sems.at[0],
                recv_sem=sems.at[1],
                device_id=(here_d, here_c, peer),
                device_id_type=MESH,
            ).start()
            return carry

        lax.fori_loop(1, nh, send, 0)

    def many(buf, count, sem):
        part = buf.at[pl.ds(0, count)]
        return pltpu.make_async_copy(part, part, sem)

    head_exchange(ri_buf, ri_sems)

    length = len_in[0]
    softmax_scale = 1.0 / math.sqrt(128)
    exp_scale = softmax_scale * math.log2(math.e)
    chunk = 256
    per = chunk // group
    start_early = here_c * rows + early
    start_late = here_c * rows + late
    start_prev = jnp.where(is_shifted, before_c * rows + half, start_early)

    def attend(at, has_prev, base, accum_k, accum_v):
        keys_from = half if has_prev else 0
        count = rows if has_prev else half
        row0 = (hq if has_prev else 0) + at * chunk
        queries = q_s[row0 : row0 + chunk]
        live = do_s[row0 : row0 + chunk]
        keys = k_s[keys_from : keys_from + count]
        values = v_s[keys_from : keys_from + count]
        scores = mm(keys, queries, NT)
        prob_grad = mm(values, live, NT)
        key_at = lax.broadcasted_iota(jnp.int32, (half, chunk), 0)
        query_at = lax.broadcasted_iota(jnp.int32, (half, chunk), 1) // group + at * per
        allowed = (key_at <= query_at) & ((key_at < length - base) | (key_at == query_at))
        if has_prev:
            allowed = jnp.concatenate([key_at < length - start_prev, allowed], axis=0)
        scores = jnp.where(allowed, scores, BLOCKED)
        top = jnp.max(scores, axis=0, keepdims=True)
        weights = jnp.exp2((scores - top) * exp_scale)
        total = jnp.sum(weights, axis=0, keepdims=True)
        query_row = lax.broadcasted_iota(jnp.int32, (1, chunk), 1) // group + at * per
        inverse = jnp.where(query_row < length - base, 1.0 / total, 0.0)
        probs = weights * inverse
        probs_low = probs.astype(BF16)
        out_dot = jnp.sum(probs_low.astype(F32) * prob_grad, axis=0, keepdims=True)
        score_grad = (probs * (prob_grad - out_dot)).astype(BF16)
        query_grad = mm(score_grad, keys, TN) * softmax_scale
        to = pl.ds(pl.multiple_of((late_q if has_prev else early_q) + at * chunk, chunk), chunk)
        dq32[to, :] = query_grad
        dq16[to, :] = query_grad.astype(BF16)
        part_k = mm(score_grad, queries, NN)
        part_v = mm(probs_low, live, NN)
        if at == 0:
            accum_k[...] = part_k
            accum_v[...] = part_v
        else:
            accum_k[...] += part_k
            accum_v[...] += part_v

    loads[4].wait()
    loads[5].wait()
    for at in range(hq // chunk):
        attend(at, False, start_early, acc_ke, acc_ve)

    for at in (6, 7, 8, 9):
        loads[at].wait()

    @pl.when(is_shifted)
    def _():
        kv_copy(k_s, 0).wait()
        kv_copy(v_s, 1).wait()

    for at in range(hq // chunk):
        attend(at, True, start_late, acc_kl, acc_vl)

    dq_copy = local(dq16, dq_out, out_sem.at[0])
    dq_copy.start()

    ret_copy = pltpu.make_async_remote_copy(
        src_ref=ret_send,
        dst_ref=ret_recv,
        send_sem=ret_sems.at[0],
        recv_sem=ret_sems.at[1],
        device_id=(here_d, before_c, here_h),
        device_id_type=MESH,
    )

    for g in range(group):
        dqcat[:, g * 128 : (g + 1) * 128] = dq32[pl.ds(g, rows, stride=group), :].astype(BF16)
    loads[10].wait()
    up_flat = jnp.concatenate(
        [u_s[...].astype(F32).reshape(rank, group, 128)[:, g, :] for g in range(group)], axis=1
    ).astype(BF16)
    rg_buf[here_h] = mm(up_flat, dqcat[...], NT)
    head_exchange(rg_buf, rg_sems)

    @pl.when(is_shifted)
    def _():
        ret_send[0:half] = acc_kl[0:half].astype(BF16)
        ret_send[half:rows] = acc_vl[0:half].astype(BF16)
        ret_copy.start()

    def scatter(part, recv, sems):
        recv[me] = part[here_c]

        def send(step, carry):
            peer = lax.rem(me + step, group_count)
            peer_c = lax.rem(peer, nc)
            pltpu.make_async_remote_copy(
                src_ref=part.at[peer_c],
                dst_ref=recv.at[me],
                send_sem=sems.at[0],
                recv_sem=sems.at[1],
                device_id=(peer // nc, peer_c, here_h),
                device_id_type=MESH,
            ).start()
            return carry

        lax.fori_loop(1, group_count, send, 0)

    def gather(recv, whole, scatter_sems, sems):
        many(recv, group_count - 1, scatter_sems.at[1]).wait()
        whole[here_c] = jnp.sum(recv[...], axis=0)

        def send(step, carry):
            pltpu.make_async_remote_copy(
                src_ref=whole.at[here_c],
                dst_ref=whole.at[here_c],
                send_sem=sems.at[0],
                recv_sem=sems.at[1],
                device_id=(here_d, lax.rem(here_c + step, nc), here_h),
                device_id_type=MESH,
            ).start()
            return carry

        lax.fori_loop(1, nc, send, 0)

    many(ri_buf, nh - 1, ri_sems.at[1]).wait()
    rank_input = jnp.sum(ri_buf[...], axis=0).astype(BF16)
    up_grad = mm(rank_input, dqcat[...], NN) * ADAPTER_SCALE
    for t in range(nc):
        up_part[t] = up_grad[:, t * 128 : (t + 1) * 128]
    scatter(up_part, up_recv, up_sems)

    many(rg_buf, nh - 1, rg_sems.at[1]).wait()
    rank_grad = jnp.sum(rg_buf[...], axis=0).astype(BF16)
    down_grad = mm(rank_grad, x_s[...], NN) * ADAPTER_SCALE
    for t in range(nc):
        dn_part[t] = down_grad[:, t * 128 : (t + 1) * 128]
    scatter(dn_part, dn_recv, dn_sems)

    gather(up_recv, up_all, up_sems, upg_sems)
    gather(dn_recv, dn_all, dn_sems, dng_sems)

    dkv_out[0, pl.ds(late_m, half), :] = (acc_kl[half:rows] * softmax_scale).astype(BF16)
    dkv_out[1, pl.ds(late_m, half), :] = acc_vl[half:rows].astype(BF16)

    @pl.when(is_shifted)
    def _():
        ret_copy.wait()
        dkv_out[0, pl.ds(early_m, half), :] = (
            (acc_ke[...] + ret_recv[0:half].astype(F32)) * softmax_scale
        ).astype(BF16)
        dkv_out[1, pl.ds(early_m, half), :] = (acc_ve[...] + ret_recv[half:rows].astype(F32)).astype(BF16)

    @pl.when(jnp.logical_not(is_shifted))
    def _():
        dkv_out[0, pl.ds(early_m, half), :] = ((acc_ke[...] + acc_kl[0:half]) * softmax_scale).astype(BF16)
        dkv_out[1, pl.ds(early_m, half), :] = (acc_ve[...] + acc_vl[0:half]).astype(BF16)

    dk_copy = local(dkv_out.at[0], dk_out, out_sem.at[1])
    dv_copy = local(dkv_out.at[1], dv_out, out_sem.at[2])
    dk_copy.start()
    dv_copy.start()

    many(up_all, nc - 1, upg_sems.at[1]).wait()
    up_whole = up_all[...]
    for r in range(rank):
        up_out[r] = up_whole[:, r, :]
    many(dn_all, nc - 1, dng_sems.at[1]).wait()
    for t in range(nc):
        down_out[:, t * 128 : (t + 1) * 128] = dn_all[t]

    many(ri_buf, nh - 1, ri_sems.at[0]).wait()
    many(rg_buf, nh - 1, rg_sems.at[0]).wait()
    many(up_recv, group_count - 1, up_sems.at[0]).wait()
    many(dn_recv, group_count - 1, dn_sems.at[0]).wait()
    many(up_all, nc - 1, upg_sems.at[0]).wait()
    many(dn_all, nc - 1, dng_sems.at[0]).wait()
    dq_copy.wait()
    dk_copy.wait()
    dv_copy.wait()


def on_device(sizes, q, k, v, do, x, adapter_down, adapter_up, lengths):
    nd, nc, nh = sizes
    rows, group, width = q.shape[1], q.shape[3], q.shape[4]
    rank, model = adapter_down.shape[1], x.shape[2]
    half = rows // 2
    dims = (nd, nc, nh, half, group, rank)
    hbm = pl.BlockSpec(memory_space=pl.ANY)
    vmem = pl.BlockSpec(memory_space=pltpu.VMEM)
    smem = pl.BlockSpec(memory_space=pltpu.SMEM)
    pair = pltpu.SemaphoreType.DMA((2,))
    tiles = (nc, rank, 128)
    all_tiles = (nd * nc, rank, 128)
    outs = pl.pallas_call(
        functools.partial(kernel, dims),
        out_shape=(
            jax.ShapeDtypeStruct((rows * group, width), BF16),
            jax.ShapeDtypeStruct((rows, width), BF16),
            jax.ShapeDtypeStruct((rows, width), BF16),
            jax.ShapeDtypeStruct((rank, model), F32),
            jax.ShapeDtypeStruct((rank, group, width), F32),
        ),
        in_specs=[hbm] * 7 + [smem],
        out_specs=(hbm, hbm, hbm, vmem, vmem),
        scratch_shapes=[
            pltpu.VMEM((rows * group, width), BF16),
            pltpu.VMEM((rows * group, width), BF16),
            pltpu.VMEM((rows, model), BF16),
            pltpu.VMEM((rank, model), BF16),
            pltpu.VMEM((rank * group, width), BF16),
            pltpu.VMEM((rows + half, width), BF16),
            pltpu.VMEM((rows + half, width), BF16),
            pltpu.VMEM((rows * group, width), F32),
            pltpu.VMEM((rows * group, width), BF16),
            pltpu.VMEM((rows, group * width), BF16),
            pltpu.VMEM((2, rows, width), BF16),
            pltpu.VMEM((half, width), F32),
            pltpu.VMEM((half, width), F32),
            pltpu.VMEM((rows, width), F32),
            pltpu.VMEM((rows, width), F32),
            pltpu.VMEM((rows, width), BF16),
            pltpu.VMEM((rows, width), BF16),
            pltpu.VMEM((nh, rank, rows), F32),
            pltpu.VMEM((nh, rank, rows), F32),
            pltpu.VMEM(tiles, F32),
            pltpu.VMEM(all_tiles, F32),
            pltpu.VMEM(tiles, F32),
            pltpu.VMEM(tiles, F32),
            pltpu.VMEM(all_tiles, F32),
            pltpu.VMEM(tiles, F32),
            pltpu.SemaphoreType.DMA((11,)),
            pltpu.SemaphoreType.DMA((3,)),
            pair, pair, pair, pair, pair, pair, pair, pair, pair,
        ],
        compiler_params=pltpu.CompilerParams(
            collective_id=0, has_side_effects=True, vmem_limit_bytes=40 * 1024 * 1024
        ),
        name="attention_and_rank_gradients",
    )(
        q.reshape(rows * group, width),
        k.reshape(rows, width),
        v.reshape(rows, width),
        do.reshape(rows * group, width),
        x.reshape(rows, model),
        adapter_down.T,
        adapter_up.reshape(rank * group, width),
        lengths,
    )
    dq, dk, dv, down, up = outs
    return (
        dq.reshape(q.shape),
        dk.reshape(k.shape),
        dv.reshape(v.shape),
        down.T,
        up.reshape(adapter_up.shape),
    )


def solution(mesh):
    sizes = (mesh.shape["dp"], mesh.shape["ctx"], mesh.shape["head"])
    return jax.shard_map(
        functools.partial(on_device, sizes),
        mesh=mesh,
        in_specs=(
            P("dp", "ctx", "head", None, None),
            P("dp", "ctx", "head", None),
            P("dp", "ctx", "head", None),
            P("dp", "ctx", "head", None, None),
            P("dp", "ctx", "head"),
            P("head", None),
            P(None, "head", None, None),
            P("dp"),
        ),
        out_specs=(
            P("dp", "ctx", "head", None, None),
            P("dp", "ctx", "head", None),
            P("dp", "ctx", "head", None),
            P("head", None),
            P(None, "head", None, None),
        ),
        check_vma=False,
    )
```

```python
import functools
import math

import jax
import jax.numpy as jnp
from jax import lax
from jax.experimental import pallas as pl
from jax.experimental.pallas import tpu as pltpu
from jax.sharding import PartitionSpec as P

ADAPTER_SCALE = 2.0
BLOCKED = -1e30
MESH = pl.DeviceIdType.MESH
F32 = jnp.float32
BF16 = jnp.bfloat16
NT = (((1,), (1,)), ((), ()))
NN = (((1,), (0,)), ((), ()))
TN = (((0,), (0,)), ((), ()))


def mm(a, b, dims):
    return lax.dot_general(a, b, dims, preferred_element_type=F32)


def kernel(
    dims,
    q_in, k_in, v_in, do_in, x_in, at_in, u_in, len_in,
    dq_out, dkv_out, down_out, up_out,
    q_s, do_s, x_s, at_s, u_s, k_s, v_s,
    dq32, dqcat, own_scores, own_grads,
    acc_ke, acc_ve, acc_kl, acc_vl, ret_send, ret_recv,
    ri_buf, rg_buf, up_a, up_ar, up_b, up_c, dn_a, dn_ar, dn_b, dn_c,
    load_sem, kv_send, kv_recv, ret_sems, ri_sems, rg_sems,
    up_asem, up_bsem, up_csem, dn_asem, dn_bsem, dn_csem,
):
    nd, nc, nh, half, group, rank = dims
    rows = 2 * half
    hq = half * group
    here_d, here_c, here_h = lax.axis_index("dp"), lax.axis_index("ctx"), lax.axis_index("head")
    core = lax.rem(here_d, 2)
    is_shifted = here_h < nh // 2
    shifted = jnp.where(is_shifted, 1, 0)
    early = shifted * half
    late = (1 - shifted) * half
    early_q = pl.multiple_of(shifted * hq, hq)
    late_q = pl.multiple_of((1 - shifted) * hq, hq)
    early_m = pl.multiple_of(early, half)
    late_m = pl.multiple_of(late, half)
    after_c = lax.rem(here_c + 1, nc)
    before_c = lax.rem(here_c + nc - 1, nc)

    def in_head(step):
        return (here_d, here_c, lax.rem(here_h + step, nh))

    def in_ctx(step):
        return (here_d, lax.rem(here_c + step, nc), here_h)

    def in_dp(step):
        return (lax.rem(here_d + step, nd), here_c, here_h)

    barrier = pltpu.get_barrier_semaphore()
    for peers, count in ((in_ctx, nc), (in_head, nh), (in_dp, nd)):
        for step in range(1, count):
            pl.semaphore_signal(barrier, inc=1, device_id=peers(step), device_id_type=MESH)

    def local(src, dst, at):
        copy = pltpu.make_async_copy(src, dst, load_sem.at[at])
        copy.start()
        return copy

    load_ke = local(k_in.at[pl.ds(early_m, half)], k_s.at[pl.ds(0, half)], 0)
    load_ve = local(v_in.at[pl.ds(early_m, half)], v_s.at[pl.ds(0, half)], 1)
    load_qe = local(q_in.at[pl.ds(early_q, hq)], q_s.at[pl.ds(0, hq)], 2)
    load_de = local(do_in.at[pl.ds(early_q, hq)], do_s.at[pl.ds(0, hq)], 3)
    load_x = local(x_in, x_s, 5)
    load_at = local(at_in, at_s, 6)
    load_kl = local(k_in.at[pl.ds(late_m, half)], k_s.at[pl.ds(rows, half)], 7)
    load_vl = local(v_in.at[pl.ds(late_m, half)], v_s.at[pl.ds(rows, half)], 8)
    load_ql = local(q_in.at[pl.ds(late_q, hq)], q_s.at[pl.ds(hq, hq)], 9)
    load_dl = local(do_in.at[pl.ds(late_q, hq)], do_s.at[pl.ds(hq, hq)], 10)
    load_u = local(u_in, u_s, 11)

    def remote(src, dst, sends, recvs, peer):
        return pltpu.make_async_remote_copy(
            src_ref=src, dst_ref=dst, send_sem=sends, recv_sem=recvs, device_id=peer, device_id_type=MESH
        )

    def many(buf, count, sem):
        part = buf.at[pl.ds(0, count)]
        return pltpu.make_async_copy(part, part, sem)

    softmax_scale = 1.0 / math.sqrt(128)
    exp_scale = softmax_scale * math.log2(math.e)
    chunk = 256
    per = chunk // group
    chunks = hq // chunk
    start_early = here_c * rows + early
    start_late = here_c * rows + late
    start_prev = jnp.where(is_shifted, before_c * rows + half, start_early)
    load_ke.wait()
    load_ve.wait()
    length = len_in[0]

    def own_part(at, keys, values, queries, live, base):
        key_at = lax.broadcasted_iota(jnp.int32, (half, chunk), 0)
        query_at = lax.broadcasted_iota(jnp.int32, (half, chunk), 1) // group + at * per
        allowed = (key_at <= query_at) & ((key_at < length - base) | (key_at == query_at))
        scores = jnp.where(allowed, mm(keys, queries, NT), BLOCKED)
        return scores, mm(values, live, NT)

    def finish(at, scores, prob_grad, keys, queries, live, base, to, accum_k, accum_v):
        top = jnp.max(scores, axis=0, keepdims=True)
        weights = jnp.exp2((scores - top) * exp_scale)
        total = jnp.sum(weights, axis=0, keepdims=True)
        query_row = lax.broadcasted_iota(jnp.int32, (1, chunk), 1) // group + at * per
        inverse = jnp.where(query_row < length - base, 1.0 / total, 0.0)
        probs = weights * inverse
        probs_low = probs.astype(BF16)
        out_dot = jnp.sum(probs_low.astype(F32) * prob_grad, axis=0, keepdims=True)
        score_grad = (probs * (prob_grad - out_dot)).astype(BF16)
        query_grad = mm(score_grad, keys, TN) * softmax_scale
        place = pl.ds(pl.multiple_of(to + at * chunk, chunk), chunk)
        dq32[place, :] = query_grad
        dq_out[place, :] = query_grad.astype(BF16)
        part_k = mm(score_grad, queries, NN)
        part_v = mm(probs_low, live, NN)
        if at == 0:
            accum_k[...] = part_k
            accum_v[...] = part_v
        else:
            accum_k[...] += part_k
            accum_v[...] += part_v

    load_qe.wait()
    load_de.wait()
    for at in range(chunks):
        queries = q_s[at * chunk : (at + 1) * chunk]
        live = do_s[at * chunk : (at + 1) * chunk]
        keys = k_s[0:half]
        scores, prob_grad = own_part(at, keys, v_s[0:half], queries, live, start_early)
        finish(at, scores, prob_grad, keys, queries, live, start_early, early_q, acc_ke, acc_ve)

    pl.semaphore_wait(barrier, nc + nh + nd - 3)

    kv_copies = [
        remote(ref.at[pl.ds(0, half)], ref.at[pl.ds(half, half)], kv_send.at[at], kv_recv.at[at], in_ctx(1))
        for at, ref in enumerate((k_s, v_s))
    ]

    @pl.when(is_shifted)
    def _():
        for copy in kv_copies:
            copy.start()

    @pl.when(jnp.logical_not(is_shifted))
    def _():
        k_s[half:rows] = k_s[0:half]
        v_s[half:rows] = v_s[0:half]

    def head_exchange(buf, sems):
        for step in range(1, nh):
            remote(buf.at[here_h], buf.at[here_h], sems.at[0], sems.at[1], in_head(step)).start()

    load_x.wait()
    load_at.wait()
    ri_buf[here_h] = mm(at_s[...], x_s[...], NT)
    head_exchange(ri_buf, ri_sems)

    load_kl.wait()
    load_vl.wait()
    load_ql.wait()
    load_dl.wait()
    for at in range(chunks):
        place = slice(hq + at * chunk, hq + (at + 1) * chunk)
        scores, prob_grad = own_part(
            at, k_s[rows : rows + half], v_s[rows : rows + half], q_s[place], do_s[place], start_late
        )
        own_scores[at] = scores
        own_grads[at] = prob_grad
    load_u.wait()
    up_flat = jnp.concatenate(
        [u_s[...].astype(F32).reshape(rank, group, 128)[:, g, :] for g in range(group)], axis=1
    ).astype(BF16)

    @pl.when(is_shifted)
    def _():
        for copy in kv_copies:
            copy.wait()

    prev_seen = lax.broadcasted_iota(jnp.int32, (half, chunk), 0) < length - start_prev
    for at in range(chunks):
        queries = q_s[hq + at * chunk : hq + (at + 1) * chunk]
        live = do_s[hq + at * chunk : hq + (at + 1) * chunk]
        prev_scores = jnp.where(prev_seen, mm(k_s[half:rows], queries, NT), BLOCKED)
        scores = jnp.concatenate([prev_scores, own_scores[at]], axis=0)
        prob_grad = jnp.concatenate([mm(v_s[half:rows], live, NT), own_grads[at]], axis=0)
        finish(
            at, scores, prob_grad, k_s[half : rows + half], queries, live, start_late, late_q, acc_kl, acc_vl
        )

    for g in range(group):
        dqcat[:, g * 128 : (g + 1) * 128] = dq32[pl.ds(g, rows, stride=group), :].astype(BF16)
    rg_buf[here_h] = mm(up_flat, dqcat[...], NT)
    head_exchange(rg_buf, rg_sems)

    ret_copy = remote(ret_send, ret_recv, ret_sems.at[0], ret_sems.at[1], in_ctx(nc - 1))

    @pl.when(is_shifted)
    def _():
        ret_send[0:half] = acc_kl[0:half].astype(BF16)
        ret_send[half:rows] = acc_vl[0:half].astype(BF16)
        ret_copy.start()

    quarter = group * 128 // 4

    def send_halves(total, part, recv, sems):
        for side in range(2):
            at = 2 * side * quarter
            part[side] = jnp.concatenate(
                [total[:, at : at + quarter], total[:, at + quarter : at + 2 * quarter]], axis=0
            ).astype(BF16)
        recv[here_d] = part[core]
        for step in range(1, nd):
            peer = in_dp(step)
            remote(part.at[lax.rem(peer[0], 2)], recv.at[here_d], sems.at[0], sems.at[1], peer).start()

    def send_over_ctx(recv, sems, onward, onward_sems):
        many(recv, nd - 1, sems.at[1]).wait()
        onward[here_c] = jnp.sum(recv[...].astype(F32), axis=0).astype(BF16)
        for step in range(1, nc):
            remote(
                onward.at[here_c], onward.at[here_c], onward_sems.at[0], onward_sems.at[1], in_ctx(step)
            ).start()

    def send_to_core(recv, sems, onward, onward_sems):
        many(recv, nc - 1, sems.at[1]).wait()
        onward[core] = jnp.sum(recv[...].astype(F32), axis=0)
        peer = (here_d + 1 - 2 * core, here_c, here_h)
        copy = remote(onward.at[core], onward.at[core], onward_sems.at[0], onward_sems.at[1], peer)
        copy.start()
        return copy

    many(ri_buf, nh - 1, ri_sems.at[1]).wait()
    rank_input = jnp.sum(ri_buf[...], axis=0).astype(BF16)
    send_halves(mm(rank_input, dqcat[...], NN) * ADAPTER_SCALE, up_a, up_ar, up_asem)

    dkv_out[0, pl.ds(late_m, half), :] = (acc_kl[half:rows] * softmax_scale).astype(BF16)
    dkv_out[1, pl.ds(late_m, half), :] = acc_vl[half:rows].astype(BF16)
    send_over_ctx(up_ar, up_asem, up_b, up_bsem)

    many(rg_buf, nh - 1, rg_sems.at[1]).wait()
    rank_grad = jnp.sum(rg_buf[...], axis=0).astype(BF16)
    send_halves(mm(rank_grad, x_s[...], NN) * ADAPTER_SCALE, dn_a, dn_ar, dn_asem)

    @pl.when(is_shifted)
    def _():
        ret_copy.wait()
        dkv_out[0, pl.ds(early_m, half), :] = (
            (acc_ke[...] + ret_recv[0:half].astype(F32)) * softmax_scale
        ).astype(BF16)
        dkv_out[1, pl.ds(early_m, half), :] = (acc_ve[...] + ret_recv[half:rows].astype(F32)).astype(BF16)

    @pl.when(jnp.logical_not(is_shifted))
    def _():
        dkv_out[0, pl.ds(early_m, half), :] = ((acc_ke[...] + acc_kl[0:half]) * softmax_scale).astype(BF16)
        dkv_out[1, pl.ds(early_m, half), :] = (acc_ve[...] + acc_vl[0:half]).astype(BF16)

    send_over_ctx(dn_ar, dn_asem, dn_b, dn_bsem)
    up_core = send_to_core(up_b, up_bsem, up_c, up_csem)
    dn_core = send_to_core(dn_b, dn_bsem, dn_c, dn_csem)

    def whole(ref):
        return jnp.concatenate(
            [ref[side, rank * row : rank * (row + 1)] for side in range(2) for row in range(2)], axis=1
        )

    up_core.wait()
    up_whole = whole(up_c)
    for g in range(group):
        up_out[:, g, :] = up_whole[:, g * 128 : (g + 1) * 128]
    for buf, count, sem in (
        (ri_buf, nh - 1, ri_sems), (rg_buf, nh - 1, rg_sems), (up_ar, nd - 1, up_asem),
        (dn_ar, nd - 1, dn_asem), (up_b, nc - 1, up_bsem), (dn_b, nc - 1, dn_bsem),
    ):
        many(buf, count, sem.at[0]).wait()
    dn_core.wait()
    down_out[...] = whole(dn_c)


def write_out(*refs):
    dq, dkv, down, up, dq_out, dk_out, dv_out, down_out, up_out, sems = refs
    pairs = ((dq, dq_out), (dkv.at[0], dk_out), (dkv.at[1], dv_out), (down, down_out), (up, up_out))
    copies = [pltpu.make_async_copy(src, dst, sems.at[at]) for at, (src, dst) in enumerate(pairs)]
    for copy in copies:
        copy.start()
    for copy in copies:
        copy.wait()


def on_device(sizes, q, k, v, do, x, adapter_down, adapter_up, lengths):
    nd, nc, nh = sizes
    rows, group, width = q.shape[1], q.shape[3], q.shape[4]
    rank, model = adapter_down.shape[1], x.shape[2]
    half = rows // 2
    hq = half * group
    dims = (nd, nc, nh, half, group, rank)
    hbm = pl.BlockSpec(memory_space=pltpu.HBM)
    anywhere = pl.BlockSpec(memory_space=pl.ANY)
    vmem = pl.BlockSpec(memory_space=pltpu.VMEM)
    pair = pltpu.SemaphoreType.DMA((2,))
    packed = (2 * rank, group * width // 4)
    results = (
        ((rows * group, width), BF16),
        ((2, rows, width), BF16),
        ((rank, model), F32),
        ((rank, group, width), F32),
    )
    operands = (
        q.reshape(rows * group, width),
        k.reshape(rows, width),
        v.reshape(rows, width),
        do.reshape(rows * group, width),
        x.reshape(rows, model),
        adapter_down.T,
        adapter_up.reshape(rank * group, width),
    )
    made = pl.pallas_call(
        functools.partial(kernel, dims),
        out_shape=tuple(pltpu.VMEM(*one) for one in results),
        in_specs=[hbm] * 7 + [pl.BlockSpec(memory_space=pltpu.SMEM)],
        out_specs=(vmem,) * 4,
        scratch_shapes=[
            pltpu.VMEM((rows * group, width), BF16),
            pltpu.VMEM((rows * group, width), BF16),
            pltpu.VMEM((rows, model), BF16),
            pltpu.VMEM((rank, model), BF16),
            pltpu.VMEM((rank * group, width), BF16),
            pltpu.VMEM((rows + half, width), BF16),
            pltpu.VMEM((rows + half, width), BF16),
            pltpu.VMEM((rows * group, width), F32),
            pltpu.VMEM((rows, group * width), BF16),
            pltpu.VMEM((hq // 256, half, 256), F32),
            pltpu.VMEM((hq // 256, half, 256), F32),
            pltpu.VMEM((half, width), F32),
            pltpu.VMEM((half, width), F32),
            pltpu.VMEM((rows, width), F32),
            pltpu.VMEM((rows, width), F32),
            pltpu.VMEM((rows, width), BF16),
            pltpu.VMEM((rows, width), BF16),
            pltpu.VMEM((nh, rank, rows), F32),
            pltpu.VMEM((nh, rank, rows), F32),
        ]
        + [
            pltpu.VMEM((2,) + packed, BF16),
            pltpu.VMEM((nd,) + packed, BF16),
            pltpu.VMEM((nc,) + packed, BF16),
            pltpu.VMEM((2,) + packed, F32),
        ]
        * 2
        + [pltpu.SemaphoreType.DMA((12,))]
        + [pair] * 11,
        compiler_params=pltpu.CompilerParams(
            collective_id=0, has_side_effects=True, vmem_limit_bytes=40 * 1024 * 1024
        ),
        name="attention_and_rank_gradients",
    )(*(pltpu.with_memory_space_constraint(one, pltpu.HBM) for one in operands), lengths)
    dq, dk, dv, down, up = pl.pallas_call(
        write_out,
        out_shape=(
            jax.ShapeDtypeStruct(*results[0]),
            jax.ShapeDtypeStruct((rows, width), BF16),
            jax.ShapeDtypeStruct((rows, width), BF16),
            jax.ShapeDtypeStruct(*results[2]),
            jax.ShapeDtypeStruct(*results[3]),
        ),
        in_specs=[anywhere] * 4,
        out_specs=(hbm,) * 5,
        scratch_shapes=[pltpu.SemaphoreType.DMA((5,))],
        name="write_results",
    )(*made)
    return (
        dq.reshape(q.shape),
        dk.reshape(k.shape),
        dv.reshape(v.shape),
        down.T,
        up.reshape(adapter_up.shape),
    )


def solution(mesh):
    sizes = (mesh.shape["dp"], mesh.shape["ctx"], mesh.shape["head"])
    return jax.shard_map(
        functools.partial(on_device, sizes),
        mesh=mesh,
        in_specs=(
            P("dp", "ctx", "head", None, None),
            P("dp", "ctx", "head", None),
            P("dp", "ctx", "head", None),
            P("dp", "ctx", "head", None, None),
            P("dp", "ctx", "head"),
            P("head", None),
            P(None, "head", None, None),
            P("dp"),
        ),
        out_specs=(
            P("dp", "ctx", "head", None, None),
            P("dp", "ctx", "head", None),
            P("dp", "ctx", "head", None),
            P("head", None),
            P(None, "head", None, None),
        ),
        check_vma=False,
    )
```

```python
import functools
import math

import jax
import jax.numpy as jnp
from jax import lax
from jax.experimental import pallas as pl
from jax.experimental.pallas import tpu as pltpu
from jax.sharding import PartitionSpec as P

ADAPTER_SCALE = 2.0
BLOCKED = -1e30
MESH = pl.DeviceIdType.MESH
F32 = jnp.float32
BF16 = jnp.bfloat16
NT = (((1,), (1,)), ((), ()))
NN = (((1,), (0,)), ((), ()))
TN = (((0,), (0,)), ((), ()))


def mm(a, b, dims):
    return lax.dot_general(a, b, dims, preferred_element_type=F32)


def kernel(
    dims,
    q_in, k_in, v_in, do_in, x_in, at_in, u_in, len_in,
    dq_out, dkv_out, down_out, up_out,
    q_s, do_s, x_s, at_s, u_s, k_s, v_s,
    dq32, dqcat, own_scores, own_grads,
    acc_ke, acc_ve, acc_kl, acc_vl, ret_send, ret_recv,
    ri_buf, rg_buf, up_a, up_ar, up_b, up_c, dn_a, dn_ar, dn_b, dn_c,
    load_sem, kv_send, kv_recv, ret_sems, ri_sems, rg_sems,
    up_asem, up_bsem, up_csem, dn_asem, dn_bsem, dn_csem,
):
    nd, nc, nh, half, group, rank = dims
    rows = 2 * half
    hq = half * group
    here_d, here_c, here_h = lax.axis_index("dp"), lax.axis_index("ctx"), lax.axis_index("head")
    core = lax.rem(here_d, 2)
    is_shifted = here_h < nh // 2
    shifted = jnp.where(is_shifted, 1, 0)
    early = shifted * half
    late = (1 - shifted) * half
    early_q = pl.multiple_of(shifted * hq, hq)
    late_q = pl.multiple_of((1 - shifted) * hq, hq)
    early_m = pl.multiple_of(early, half)
    late_m = pl.multiple_of(late, half)
    after_c = lax.rem(here_c + 1, nc)
    before_c = lax.rem(here_c + nc - 1, nc)

    def in_head(step):
        return (here_d, here_c, lax.rem(here_h + step, nh))

    def in_ctx(step):
        return (here_d, lax.rem(here_c + step, nc), here_h)

    def in_dp(step):
        return (lax.rem(here_d + step, nd), here_c, here_h)

    barrier = pltpu.get_barrier_semaphore()
    for peers, count in ((in_ctx, nc), (in_head, nh), (in_dp, nd)):
        for step in range(1, count):
            pl.semaphore_signal(barrier, inc=1, device_id=peers(step), device_id_type=MESH)

    def local(src, dst, at):
        copy = pltpu.make_async_copy(src, dst, load_sem.at[at])
        copy.start()
        return copy

    load_ke = local(k_in.at[pl.ds(early_m, half)], k_s.at[pl.ds(0, half)], 0)
    load_ve = local(v_in.at[pl.ds(early_m, half)], v_s.at[pl.ds(0, half)], 1)
    load_qe = local(q_in.at[pl.ds(early_q, hq)], q_s.at[pl.ds(0, hq)], 2)
    load_de = local(do_in.at[pl.ds(early_q, hq)], do_s.at[pl.ds(0, hq)], 3)
    load_x = local(x_in, x_s, 5)
    load_at = local(at_in, at_s, 6)
    load_kl = local(k_in.at[pl.ds(late_m, half)], k_s.at[pl.ds(rows, half)], 7)
    load_vl = local(v_in.at[pl.ds(late_m, half)], v_s.at[pl.ds(rows, half)], 8)
    load_ql = local(q_in.at[pl.ds(late_q, hq)], q_s.at[pl.ds(hq, hq)], 9)
    load_dl = local(do_in.at[pl.ds(late_q, hq)], do_s.at[pl.ds(hq, hq)], 10)
    load_u = local(u_in, u_s, 11)

    def remote(src, dst, sends, recvs, peer):
        return pltpu.make_async_remote_copy(
            src_ref=src, dst_ref=dst, send_sem=sends, recv_sem=recvs, device_id=peer, device_id_type=MESH
        )

    def many(buf, count, sem):
        part = buf.at[pl.ds(0, count)]
        return pltpu.make_async_copy(part, part, sem)

    softmax_scale = 1.0 / math.sqrt(128)
    exp_scale = softmax_scale * math.log2(math.e)
    chunk = 256
    per = chunk // group
    chunks = hq // chunk
    start_early = here_c * rows + early
    start_late = here_c * rows + late
    start_prev = jnp.where(is_shifted, before_c * rows + half, start_early)
    load_ke.wait()
    load_ve.wait()
    length = len_in[0]

    def own_part(at, keys, values, queries, live, base):
        key_at = lax.broadcasted_iota(jnp.int32, (half, chunk), 0)
        query_at = lax.broadcasted_iota(jnp.int32, (half, chunk), 1) // group + at * per
        allowed = (key_at <= query_at) & ((key_at < length - base) | (key_at == query_at))
        scores = jnp.where(allowed, mm(keys, queries, NT), BLOCKED)
        return scores, mm(values, live, NT)

    def finish(at, scores, prob_grad, keys, queries, live, base, to, accum_k, accum_v):
        top = jnp.max(scores, axis=0, keepdims=True)
        weights = jnp.exp2((scores - top) * exp_scale)
        total = jnp.sum(weights, axis=0, keepdims=True)
        query_row = lax.broadcasted_iota(jnp.int32, (1, chunk), 1) // group + at * per
        inverse = jnp.where(query_row < length - base, 1.0 / total, 0.0)
        probs = weights * inverse
        probs_low = probs.astype(BF16)
        out_dot = jnp.sum(probs_low.astype(F32) * prob_grad, axis=0, keepdims=True)
        score_grad = (probs * (prob_grad - out_dot)).astype(BF16)
        query_grad = mm(score_grad, keys, TN) * softmax_scale
        place = pl.ds(pl.multiple_of(to + at * chunk, chunk), chunk)
        dq32[place, :] = query_grad
        dq_out[place, :] = query_grad.astype(BF16)
        part_k = mm(score_grad, queries, NN)
        part_v = mm(probs_low, live, NN)
        if at == 0:
            accum_k[...] = part_k
            accum_v[...] = part_v
        else:
            accum_k[...] += part_k
            accum_v[...] += part_v

    load_qe.wait()
    load_de.wait()
    for at in range(chunks):
        queries = q_s[at * chunk : (at + 1) * chunk]
        live = do_s[at * chunk : (at + 1) * chunk]
        keys = k_s[0:half]
        scores, prob_grad = own_part(at, keys, v_s[0:half], queries, live, start_early)
        finish(at, scores, prob_grad, keys, queries, live, start_early, early_q, acc_ke, acc_ve)

    pl.semaphore_wait(barrier, nc + nh + nd - 3)

    kv_copies = [
        remote(ref.at[pl.ds(0, half)], ref.at[pl.ds(half, half)], kv_send.at[at], kv_recv.at[at], in_ctx(1))
        for at, ref in enumerate((k_s, v_s))
    ]

    @pl.when(is_shifted)
    def _():
        for copy in kv_copies:
            copy.start()

    @pl.when(jnp.logical_not(is_shifted))
    def _():
        k_s[half:rows] = k_s[0:half]
        v_s[half:rows] = v_s[0:half]

    def head_exchange(buf, sems):
        for step in range(1, nh):
            remote(buf.at[here_h], buf.at[here_h], sems.at[0], sems.at[1], in_head(step)).start()

    load_x.wait()
    load_at.wait()
    ri_buf[here_h] = mm(at_s[...], x_s[...], NT)
    head_exchange(ri_buf, ri_sems)

    load_kl.wait()
    load_vl.wait()
    load_ql.wait()
    load_dl.wait()
    for at in range(chunks):
        place = slice(hq + at * chunk, hq + (at + 1) * chunk)
        scores, prob_grad = own_part(
            at, k_s[rows : rows + half], v_s[rows : rows + half], q_s[place], do_s[place], start_late
        )
        own_scores[at] = scores
        own_grads[at] = prob_grad
    load_u.wait()
    up_flat = jnp.concatenate(
        [u_s[...].astype(F32).reshape(rank, group, 128)[:, g, :] for g in range(group)], axis=1
    ).astype(BF16)

    @pl.when(is_shifted)
    def _():
        for copy in kv_copies:
            copy.wait()

    prev_seen = lax.broadcasted_iota(jnp.int32, (half, chunk), 0) < length - start_prev
    for at in range(chunks):
        queries = q_s[hq + at * chunk : hq + (at + 1) * chunk]
        live = do_s[hq + at * chunk : hq + (at + 1) * chunk]
        prev_scores = jnp.where(prev_seen, mm(k_s[half:rows], queries, NT), BLOCKED)
        scores = jnp.concatenate([prev_scores, own_scores[at]], axis=0)
        prob_grad = jnp.concatenate([mm(v_s[half:rows], live, NT), own_grads[at]], axis=0)
        finish(
            at, scores, prob_grad, k_s[half : rows + half], queries, live, start_late, late_q, acc_kl, acc_vl
        )

    for g in range(group):
        dqcat[:, g * 128 : (g + 1) * 128] = dq32[pl.ds(g, rows, stride=group), :].astype(BF16)
    rg_buf[here_h] = mm(up_flat, dqcat[...], NT)
    head_exchange(rg_buf, rg_sems)

    ret_copy = remote(ret_send, ret_recv, ret_sems.at[0], ret_sems.at[1], in_ctx(nc - 1))

    @pl.when(is_shifted)
    def _():
        ret_send[0:half] = acc_kl[0:half].astype(BF16)
        ret_send[half:rows] = acc_vl[0:half].astype(BF16)
        ret_copy.start()

    quarter = group * 128 // 4

    def send_halves(total, part, recv, sems):
        for side in range(2):
            at = 2 * side * quarter
            part[side] = jnp.concatenate(
                [total[:, at : at + quarter], total[:, at + quarter : at + 2 * quarter]], axis=0
            ).astype(BF16)
        recv[here_d] = part[core]
        for step in range(1, nd):
            peer = in_dp(step)
            remote(part.at[lax.rem(peer[0], 2)], recv.at[here_d], sems.at[0], sems.at[1], peer).start()

    def send_over_ctx(recv, sems, onward, onward_sems):
        many(recv, nd - 1, sems.at[1]).wait()
        onward[here_c] = jnp.sum(recv[...].astype(F32), axis=0).astype(BF16)
        for step in range(1, nc):
            remote(
                onward.at[here_c], onward.at[here_c], onward_sems.at[0], onward_sems.at[1], in_ctx(step)
            ).start()

    def send_to_core(recv, sems, onward, onward_sems):
        many(recv, nc - 1, sems.at[1]).wait()
        onward[core] = jnp.sum(recv[...].astype(F32), axis=0)
        peer = (here_d + 1 - 2 * core, here_c, here_h)
        copy = remote(onward.at[core], onward.at[core], onward_sems.at[0], onward_sems.at[1], peer)
        copy.start()
        return copy

    many(ri_buf, nh - 1, ri_sems.at[1]).wait()
    rank_input = jnp.sum(ri_buf[...], axis=0).astype(BF16)
    send_halves(mm(rank_input, dqcat[...], NN) * ADAPTER_SCALE, up_a, up_ar, up_asem)

    dkv_out[0, pl.ds(late_m, half), :] = (acc_kl[half:rows] * softmax_scale).astype(BF16)
    dkv_out[1, pl.ds(late_m, half), :] = acc_vl[half:rows].astype(BF16)
    send_over_ctx(up_ar, up_asem, up_b, up_bsem)

    many(rg_buf, nh - 1, rg_sems.at[1]).wait()
    rank_grad = jnp.sum(rg_buf[...], axis=0).astype(BF16)
    send_halves(mm(rank_grad, x_s[...], NN) * ADAPTER_SCALE, dn_a, dn_ar, dn_asem)

    @pl.when(is_shifted)
    def _():
        ret_copy.wait()
        dkv_out[0, pl.ds(early_m, half), :] = (
            (acc_ke[...] + ret_recv[0:half].astype(F32)) * softmax_scale
        ).astype(BF16)
        dkv_out[1, pl.ds(early_m, half), :] = (acc_ve[...] + ret_recv[half:rows].astype(F32)).astype(BF16)

    @pl.when(jnp.logical_not(is_shifted))
    def _():
        dkv_out[0, pl.ds(early_m, half), :] = ((acc_ke[...] + acc_kl[0:half]) * softmax_scale).astype(BF16)
        dkv_out[1, pl.ds(early_m, half), :] = (acc_ve[...] + acc_vl[0:half]).astype(BF16)

    send_over_ctx(dn_ar, dn_asem, dn_b, dn_bsem)
    up_core = send_to_core(up_b, up_bsem, up_c, up_csem)
    dn_core = send_to_core(dn_b, dn_bsem, dn_c, dn_csem)

    def whole(ref):
        return jnp.concatenate(
            [ref[side, rank * row : rank * (row + 1)] for side in range(2) for row in range(2)], axis=1
        )

    up_core.wait()
    up_whole = whole(up_c)
    for g in range(group):
        up_out[:, g, :] = up_whole[:, g * 128 : (g + 1) * 128]
    for buf, count, sem in (
        (ri_buf, nh - 1, ri_sems), (rg_buf, nh - 1, rg_sems), (up_ar, nd - 1, up_asem),
        (dn_ar, nd - 1, dn_asem), (up_b, nc - 1, up_bsem), (dn_b, nc - 1, dn_bsem),
    ):
        many(buf, count, sem.at[0]).wait()
    dn_core.wait()
    down_out[...] = whole(dn_c)


def write_out(*refs):
    dq, dkv, down, up, dq_out, dk_out, dv_out, down_out, up_out, sems = refs
    pairs = ((dq, dq_out), (dkv.at[0], dk_out), (dkv.at[1], dv_out), (down, down_out), (up, up_out))
    copies = [pltpu.make_async_copy(src, dst, sems.at[at]) for at, (src, dst) in enumerate(pairs)]
    for copy in copies:
        copy.start()
    for copy in copies:
        copy.wait()


def on_device(sizes, q, k, v, do, x, adapter_down, adapter_up, lengths):
    nd, nc, nh = sizes
    rows, group, width = q.shape[1], q.shape[3], q.shape[4]
    rank, model = adapter_down.shape[1], x.shape[2]
    half = rows // 2
    hq = half * group
    dims = (nd, nc, nh, half, group, rank)
    hbm = pl.BlockSpec(memory_space=pltpu.HBM)
    vmem = pl.BlockSpec(memory_space=pltpu.VMEM)
    pair = pltpu.SemaphoreType.DMA((2,))
    packed = (2 * rank, group * width // 4)
    results = (
        ((rows * group, width), BF16),
        ((2, rows, width), BF16),
        ((rank, model), F32),
        ((rank, group, width), F32),
    )
    operands = (
        q.reshape(rows * group, width),
        k.reshape(rows, width),
        v.reshape(rows, width),
        do.reshape(rows * group, width),
        x.reshape(rows, model),
        adapter_down.T,
        adapter_up.reshape(rank * group, width),
    )
    made = pl.pallas_call(
        functools.partial(kernel, dims),
        out_shape=tuple(pltpu.VMEM(*one) for one in results),
        in_specs=[hbm] * 7 + [pl.BlockSpec(memory_space=pltpu.SMEM)],
        out_specs=(vmem,) * 4,
        scratch_shapes=[
            pltpu.VMEM((rows * group, width), BF16),
            pltpu.VMEM((rows * group, width), BF16),
            pltpu.VMEM((rows, model), BF16),
            pltpu.VMEM((rank, model), BF16),
            pltpu.VMEM((rank * group, width), BF16),
            pltpu.VMEM((rows + half, width), BF16),
            pltpu.VMEM((rows + half, width), BF16),
            pltpu.VMEM((rows * group, width), F32),
            pltpu.VMEM((rows, group * width), BF16),
            pltpu.VMEM((hq // 256, half, 256), F32),
            pltpu.VMEM((hq // 256, half, 256), F32),
            pltpu.VMEM((half, width), F32),
            pltpu.VMEM((half, width), F32),
            pltpu.VMEM((rows, width), F32),
            pltpu.VMEM((rows, width), F32),
            pltpu.VMEM((rows, width), BF16),
            pltpu.VMEM((rows, width), BF16),
            pltpu.VMEM((nh, rank, rows), F32),
            pltpu.VMEM((nh, rank, rows), F32),
        ]
        + [
            pltpu.VMEM((2,) + packed, BF16),
            pltpu.VMEM((nd,) + packed, BF16),
            pltpu.VMEM((nc,) + packed, BF16),
            pltpu.VMEM((2,) + packed, F32),
        ]
        * 2
        + [pltpu.SemaphoreType.DMA((12,))]
        + [pair] * 11,
        compiler_params=pltpu.CompilerParams(
            collective_id=0, has_side_effects=True, vmem_limit_bytes=40 * 1024 * 1024
        ),
        name="attention_and_rank_gradients",
    )(*(pltpu.with_memory_space_constraint(one, pltpu.HBM) for one in operands), lengths)
    dq, dk, dv, down, up = pl.pallas_call(
        write_out,
        out_shape=(
            jax.ShapeDtypeStruct(*results[0]),
            jax.ShapeDtypeStruct((rows, width), BF16),
            jax.ShapeDtypeStruct((rows, width), BF16),
            jax.ShapeDtypeStruct(*results[2]),
            jax.ShapeDtypeStruct(*results[3]),
        ),
        in_specs=[vmem] * 4,
        out_specs=(hbm,) * 5,
        scratch_shapes=[pltpu.SemaphoreType.DMA((5,))],
        name="write_results",
    )(*(pltpu.with_memory_space_constraint(one, pltpu.VMEM) for one in made))
    return (
        dq.reshape(q.shape),
        dk.reshape(k.shape),
        dv.reshape(v.shape),
        down.T,
        up.reshape(adapter_up.shape),
    )


def solution(mesh):
    sizes = (mesh.shape["dp"], mesh.shape["ctx"], mesh.shape["head"])
    return jax.shard_map(
        functools.partial(on_device, sizes),
        mesh=mesh,
        in_specs=(
            P("dp", "ctx", "head", None, None),
            P("dp", "ctx", "head", None),
            P("dp", "ctx", "head", None),
            P("dp", "ctx", "head", None, None),
            P("dp", "ctx", "head"),
            P("head", None),
            P(None, "head", None, None),
            P("dp"),
        ),
        out_specs=(
            P("dp", "ctx", "head", None, None),
            P("dp", "ctx", "head", None),
            P("dp", "ctx", "head", None),
            P("head", None),
            P(None, "head", None, None),
        ),
        check_vma=False,
    )
```

```python
import functools
import math

import jax
import jax.numpy as jnp
from jax import lax
from jax.experimental import pallas as pl
from jax.experimental.pallas import tpu as pltpu
from jax.sharding import PartitionSpec as P

ADAPTER_SCALE = 2.0
BLOCKED = -1e30
CHUNK = 256
MESH = pl.DeviceIdType.MESH
F32 = jnp.float32
BF16 = jnp.bfloat16
NT = (((1,), (1,)), ((), ()))
NN = (((1,), (0,)), ((), ()))
TN = (((0,), (0,)), ((), ()))


def far_first(count):
    return sorted(range(1, count), key=lambda step: -min(step, count - step))


def mm(a, b, dims):
    return lax.dot_general(a, b, dims, preferred_element_type=F32)


def kernel(
    dims,
    q_in, k_in, v_in, do_in, x_in, at_in, u_in, len_in,
    dq_out, dkv_out, down_out, up_out,
    q_s, do_s, x_s, at_s, u_s, k_s, v_s,
    dq32, dqcat, own_scores, own_grads,
    acc_ke, acc_ve, acc_kl, acc_vl, ret_send, ret_recv,
    ri_buf, rg_buf, up_a, up_b, dn_a, dn_b,
    load_sem, kv_send, kv_recv, ret_sems, ri_sems, rg_sems,
    up_asem, up_bsem, dn_asem, dn_bsem,
):
    nd, nc, nh, half, group, rank = dims
    rows = 2 * half
    hq = half * group
    here_d, here_c, here_h = lax.axis_index("dp"), lax.axis_index("ctx"), lax.axis_index("head")
    is_shifted = here_h < nh // 2
    shifted = jnp.where(is_shifted, 1, 0)
    early = shifted * half
    late = (1 - shifted) * half
    early_q = pl.multiple_of(shifted * hq, hq)
    late_q = pl.multiple_of((1 - shifted) * hq, hq)
    early_m = pl.multiple_of(early, half)
    late_m = pl.multiple_of(late, half)
    after_c = lax.rem(here_c + 1, nc)
    before_c = lax.rem(here_c + nc - 1, nc)

    def in_head(step):
        return (here_d, here_c, lax.rem(here_h + step, nh))

    def in_ctx(step):
        return (here_d, lax.rem(here_c + step, nc), here_h)

    def in_dp(step):
        return (lax.rem(here_d + step, nd), here_c, here_h)

    barrier = pltpu.get_barrier_semaphore()
    for peers, count in ((in_ctx, nc), (in_head, nh), (in_dp, nd)):
        for step in far_first(count):
            pl.semaphore_signal(barrier, inc=1, device_id=peers(step), device_id_type=MESH)

    def local(src, dst, at):
        copy = pltpu.make_async_copy(src, dst, load_sem.at[at])
        copy.start()
        return copy

    load_ke = local(k_in.at[pl.ds(early_m, half)], k_s.at[pl.ds(0, half)], 0)
    load_ve = local(v_in.at[pl.ds(early_m, half)], v_s.at[pl.ds(0, half)], 1)
    load_qe = local(q_in.at[pl.ds(early_q, hq)], q_s.at[pl.ds(0, hq)], 2)
    load_de = local(do_in.at[pl.ds(early_q, hq)], do_s.at[pl.ds(0, hq)], 3)
    load_x = local(x_in, x_s, 5)
    load_at = local(at_in, at_s, 6)
    load_kl = local(k_in.at[pl.ds(late_m, half)], k_s.at[pl.ds(rows, half)], 7)
    load_vl = local(v_in.at[pl.ds(late_m, half)], v_s.at[pl.ds(rows, half)], 8)
    load_ql = local(q_in.at[pl.ds(late_q, hq)], q_s.at[pl.ds(hq, hq)], 9)
    load_dl = local(do_in.at[pl.ds(late_q, hq)], do_s.at[pl.ds(hq, hq)], 10)
    load_u = local(u_in, u_s, 11)

    def remote(src, dst, sends, recvs, peer):
        return pltpu.make_async_remote_copy(
            src_ref=src, dst_ref=dst, send_sem=sends, recv_sem=recvs, device_id=peer, device_id_type=MESH
        )

    def many(buf, count, sem):
        part = buf.at[pl.ds(0, count)]
        return pltpu.make_async_copy(part, part, sem)

    softmax_scale = 1.0 / math.sqrt(128)
    exp_scale = softmax_scale * math.log2(math.e)
    chunk = CHUNK
    per = chunk // group
    chunks = hq // chunk
    start_early = here_c * rows + early
    start_late = here_c * rows + late
    start_prev = jnp.where(is_shifted, before_c * rows + half, start_early)
    load_ke.wait()
    load_ve.wait()
    length = len_in[...]

    def own_part(at, keys, values, queries, live, base):
        key_at = lax.broadcasted_iota(jnp.int32, (half, chunk), 0)
        query_at = lax.broadcasted_iota(jnp.int32, (half, chunk), 1) // group + at * per
        allowed = (key_at <= query_at) & ((key_at < length - base) | (key_at == query_at))
        scores = jnp.where(allowed, mm(keys, queries, NT), BLOCKED)
        return scores, mm(values, live, NT)

    def finish(at, scores, prob_grad, keys, queries, live, base, to, accum_k, accum_v):
        top = jnp.max(scores, axis=0, keepdims=True)
        weights = jnp.exp2((scores - top) * exp_scale)
        total = jnp.sum(weights, axis=0, keepdims=True)
        query_row = lax.broadcasted_iota(jnp.int32, (1, chunk), 1) // group + at * per
        inverse = jnp.where(query_row < length - base, 1.0 / total, 0.0)
        probs = weights * inverse
        probs_low = probs.astype(BF16)
        out_dot = jnp.sum(probs_low.astype(F32) * prob_grad, axis=0, keepdims=True)
        score_grad = (probs * (prob_grad - out_dot)).astype(BF16)
        query_grad = mm(score_grad, keys, TN) * softmax_scale
        place = pl.ds(pl.multiple_of(to + at * chunk, chunk), chunk)
        dq32[place, :] = query_grad
        dq_out[place, :] = query_grad.astype(BF16)
        part_k = mm(score_grad, queries, NN)
        part_v = mm(probs_low, live, NN)
        if at == 0:
            accum_k[...] = part_k
            accum_v[...] = part_v
        else:
            accum_k[...] += part_k
            accum_v[...] += part_v

    load_qe.wait()
    load_de.wait()
    for at in range(chunks):
        queries = q_s[at * chunk : (at + 1) * chunk]
        live = do_s[at * chunk : (at + 1) * chunk]
        keys = k_s[0:half]
        scores, prob_grad = own_part(at, keys, v_s[0:half], queries, live, start_early)
        finish(at, scores, prob_grad, keys, queries, live, start_early, early_q, acc_ke, acc_ve)

    pl.semaphore_wait(barrier, nc + nh + nd - 3)

    kv_copies = [
        remote(ref.at[pl.ds(0, half)], ref.at[pl.ds(half, half)], kv_send.at[at], kv_recv.at[at], in_ctx(1))
        for at, ref in enumerate((k_s, v_s))
    ]

    @pl.when(is_shifted)
    def _():
        for copy in kv_copies:
            copy.start()

    @pl.when(jnp.logical_not(is_shifted))
    def _():
        k_s[half:rows] = k_s[0:half]
        v_s[half:rows] = v_s[0:half]

    def head_exchange(buf, sems):
        for step in far_first(nh):
            remote(buf.at[here_h], buf.at[here_h], sems.at[0], sems.at[1], in_head(step)).start()

    load_x.wait()
    load_at.wait()
    ri_buf[here_h] = mm(at_s[...], x_s[...], NT)
    head_exchange(ri_buf, ri_sems)

    load_kl.wait()
    load_vl.wait()
    load_ql.wait()
    load_dl.wait()
    for at in range(chunks):
        place = slice(hq + at * chunk, hq + (at + 1) * chunk)
        scores, prob_grad = own_part(
            at, k_s[rows : rows + half], v_s[rows : rows + half], q_s[place], do_s[place], start_late
        )
        own_scores[at] = scores
        own_grads[at] = prob_grad
    load_u.wait()
    up_flat = jnp.concatenate(
        [u_s[...].astype(F32).reshape(rank, group, 128)[:, g, :] for g in range(group)], axis=1
    ).astype(BF16)

    @pl.when(is_shifted)
    def _():
        for copy in kv_copies:
            copy.wait()

    prev_seen = lax.broadcasted_iota(jnp.int32, (half, chunk), 0) < length - start_prev
    for at in range(chunks):
        queries = q_s[hq + at * chunk : hq + (at + 1) * chunk]
        live = do_s[hq + at * chunk : hq + (at + 1) * chunk]
        prev_scores = jnp.where(prev_seen, mm(k_s[half:rows], queries, NT), BLOCKED)
        scores = jnp.concatenate([prev_scores, own_scores[at]], axis=0)
        prob_grad = jnp.concatenate([mm(v_s[half:rows], live, NT), own_grads[at]], axis=0)
        finish(
            at, scores, prob_grad, k_s[half : rows + half], queries, live, start_late, late_q, acc_kl, acc_vl
        )

    for g in range(group):
        dqcat[:, g * 128 : (g + 1) * 128] = dq32[pl.ds(g, rows, stride=group), :].astype(BF16)
    rg_buf[here_h] = mm(up_flat, dqcat[...], NT)
    head_exchange(rg_buf, rg_sems)

    ret_copy = remote(ret_send, ret_recv, ret_sems.at[0], ret_sems.at[1], in_ctx(nc - 1))

    @pl.when(is_shifted)
    def _():
        ret_send[0:half] = acc_kl[0:half].astype(BF16)
        ret_send[half:rows] = acc_vl[0:half].astype(BF16)
        ret_copy.start()

    wide = group * 128 // 2

    def send_over_dp(total, recv, sems):
        recv[here_d] = jnp.concatenate([total[:, :wide], total[:, wide:]], axis=0).astype(BF16)
        for step in range(nd - 1, 0, -1):
            remote(recv.at[here_d], recv.at[here_d], sems.at[0], sems.at[1], in_dp(step)).start()

    def send_over_ctx(recv, sems, onward, onward_sems):
        many(recv, nd - 1, sems.at[1]).wait()
        onward[here_c] = jnp.sum(recv[...].astype(F32), axis=0).astype(BF16)
        for step in far_first(nc):
            remote(
                onward.at[here_c], onward.at[here_c], onward_sems.at[0], onward_sems.at[1], in_ctx(step)
            ).start()

    def whole(recv, sems):
        many(recv, nc - 1, sems.at[1]).wait()
        total = jnp.sum(recv[...].astype(F32), axis=0)
        return jnp.concatenate([total[:rank], total[rank:]], axis=1)

    many(ri_buf, nh - 1, ri_sems.at[1]).wait()
    rank_input = jnp.sum(ri_buf[...], axis=0).astype(BF16)
    send_over_dp(mm(rank_input, dqcat[...], NN) * ADAPTER_SCALE, up_a, up_asem)

    dkv_out[0, pl.ds(late_m, half), :] = (acc_kl[half:rows] * softmax_scale).astype(BF16)
    dkv_out[1, pl.ds(late_m, half), :] = acc_vl[half:rows].astype(BF16)
    send_over_ctx(up_a, up_asem, up_b, up_bsem)

    many(rg_buf, nh - 1, rg_sems.at[1]).wait()
    rank_grad = jnp.sum(rg_buf[...], axis=0).astype(BF16)
    send_over_dp(mm(rank_grad, x_s[...], NN) * ADAPTER_SCALE, dn_a, dn_asem)

    @pl.when(is_shifted)
    def _():
        ret_copy.wait()
        dkv_out[0, pl.ds(early_m, half), :] = (
            (acc_ke[...] + ret_recv[0:half].astype(F32)) * softmax_scale
        ).astype(BF16)
        dkv_out[1, pl.ds(early_m, half), :] = (acc_ve[...] + ret_recv[half:rows].astype(F32)).astype(BF16)

    @pl.when(jnp.logical_not(is_shifted))
    def _():
        dkv_out[0, pl.ds(early_m, half), :] = ((acc_ke[...] + acc_kl[0:half]) * softmax_scale).astype(BF16)
        dkv_out[1, pl.ds(early_m, half), :] = (acc_ve[...] + acc_vl[0:half]).astype(BF16)

    send_over_ctx(dn_a, dn_asem, dn_b, dn_bsem)
    up_whole = whole(up_b, up_bsem)
    for g in range(group):
        up_out[:, g, :] = up_whole[:, g * 128 : (g + 1) * 128]
    for buf, count, sem in (
        (ri_buf, nh - 1, ri_sems), (rg_buf, nh - 1, rg_sems), (up_a, nd - 1, up_asem),
        (dn_a, nd - 1, dn_asem), (up_b, nc - 1, up_bsem), (dn_b, nc - 1, dn_bsem),
    ):
        many(buf, count, sem.at[0]).wait()
    down_out[...] = whole(dn_b, dn_bsem)


def write_out(*refs):
    dq, dkv, down, up, dq_out, dk_out, dv_out, down_out, up_out, sems = refs
    pairs = ((dq, dq_out), (dkv.at[0], dk_out), (dkv.at[1], dv_out), (down, down_out), (up, up_out))
    copies = [pltpu.make_async_copy(src, dst, sems.at[at]) for at, (src, dst) in enumerate(pairs)]
    for copy in copies:
        copy.start()
    for copy in copies:
        copy.wait()


def on_device(sizes, q, k, v, do, x, adapter_down, adapter_up, lengths):
    nd, nc, nh = sizes
    rows, group, width = q.shape[1], q.shape[3], q.shape[4]
    rank, model = adapter_down.shape[1], x.shape[2]
    half = rows // 2
    hq = half * group
    dims = (nd, nc, nh, half, group, rank)
    hbm = pl.BlockSpec(memory_space=pltpu.HBM)
    vmem = pl.BlockSpec(memory_space=pltpu.VMEM)
    pair = pltpu.SemaphoreType.DMA((2,))
    packed = (2 * rank, group * width // 2)
    results = (
        ((rows * group, width), BF16),
        ((2, rows, width), BF16),
        ((rank, model), F32),
        ((rank, group, width), F32),
    )
    operands = (
        q.reshape(rows * group, width),
        k.reshape(rows, width),
        v.reshape(rows, width),
        do.reshape(rows * group, width),
        x.reshape(rows, model),
        adapter_down.T,
        adapter_up.reshape(rank * group, width),
    )
    made = pl.pallas_call(
        functools.partial(kernel, dims),
        out_shape=tuple(pltpu.VMEM(*one) for one in results),
        in_specs=[hbm] * 7 + [vmem],
        out_specs=(vmem,) * 4,
        scratch_shapes=[
            pltpu.VMEM((rows * group, width), BF16),
            pltpu.VMEM((rows * group, width), BF16),
            pltpu.VMEM((rows, model), BF16),
            pltpu.VMEM((rank, model), BF16),
            pltpu.VMEM((rank * group, width), BF16),
            pltpu.VMEM((rows + half, width), BF16),
            pltpu.VMEM((rows + half, width), BF16),
            pltpu.VMEM((rows * group, width), F32),
            pltpu.VMEM((rows, group * width), BF16),
            pltpu.VMEM((hq // CHUNK, half, CHUNK), F32),
            pltpu.VMEM((hq // CHUNK, half, CHUNK), F32),
            pltpu.VMEM((half, width), F32),
            pltpu.VMEM((half, width), F32),
            pltpu.VMEM((rows, width), F32),
            pltpu.VMEM((rows, width), F32),
            pltpu.VMEM((rows, width), BF16),
            pltpu.VMEM((rows, width), BF16),
            pltpu.VMEM((nh, rank, rows), F32),
            pltpu.VMEM((nh, rank, rows), F32),
        ]
        + [
            pltpu.VMEM((nd,) + packed, BF16),
            pltpu.VMEM((nc,) + packed, BF16),
        ]
        * 2
        + [pltpu.SemaphoreType.DMA((12,))]
        + [pair] * 9,
        compiler_params=pltpu.CompilerParams(
            collective_id=0, has_side_effects=True, vmem_limit_bytes=40 * 1024 * 1024
        ),
        name="attention_and_rank_gradients",
    )(
        *(pltpu.with_memory_space_constraint(one, pltpu.HBM) for one in operands),
        pltpu.with_memory_space_constraint(jnp.broadcast_to(lengths[:, None], (1, CHUNK)), pltpu.VMEM),
    )
    dq, dk, dv, down, up = pl.pallas_call(
        write_out,
        out_shape=(
            jax.ShapeDtypeStruct(*results[0]),
            jax.ShapeDtypeStruct((rows, width), BF16),
            jax.ShapeDtypeStruct((rows, width), BF16),
            jax.ShapeDtypeStruct(*results[2]),
            jax.ShapeDtypeStruct(*results[3]),
        ),
        in_specs=[vmem] * 4,
        out_specs=(hbm,) * 5,
        scratch_shapes=[pltpu.SemaphoreType.DMA((5,))],
        name="write_results",
    )(*(pltpu.with_memory_space_constraint(one, pltpu.VMEM) for one in made))
    return (
        dq.reshape(q.shape),
        dk.reshape(k.shape),
        dv.reshape(v.shape),
        down.T,
        up.reshape(adapter_up.shape),
    )


def solution(mesh):
    sizes = (mesh.shape["dp"], mesh.shape["ctx"], mesh.shape["head"])
    return jax.shard_map(
        functools.partial(on_device, sizes),
        mesh=mesh,
        in_specs=(
            P("dp", "ctx", "head", None, None),
            P("dp", "ctx", "head", None),
            P("dp", "ctx", "head", None),
            P("dp", "ctx", "head", None, None),
            P("dp", "ctx", "head"),
            P("head", None),
            P(None, "head", None, None),
            P("dp"),
        ),
        out_specs=(
            P("dp", "ctx", "head", None, None),
            P("dp", "ctx", "head", None),
            P("dp", "ctx", "head", None),
            P("head", None),
            P(None, "head", None, None),
        ),
        check_vma=False,
    )
```

```python
import functools
import math

import jax
import jax.numpy as jnp
from jax import lax
from jax.experimental import pallas as pl
from jax.experimental.pallas import tpu as pltpu
from jax.sharding import PartitionSpec as P

ADAPTER_SCALE = 2.0
BLOCKED = -1e30
CHUNK = 256
MESH = pl.DeviceIdType.MESH
F32 = jnp.float32
BF16 = jnp.bfloat16
NT = (((1,), (1,)), ((), ()))
NN = (((1,), (0,)), ((), ()))
TN = (((0,), (0,)), ((), ()))


def far_first(count):
    return sorted(range(1, count), key=lambda step: -min(step, count - step))


def mm(a, b, dims):
    return lax.dot_general(a, b, dims, preferred_element_type=F32)


def kernel(
    dims,
    q_in, k_in, v_in, do_in, x_in, at_in, u_in, len_in,
    dq_out, dkv_out, down_out, up_out,
    q_s, do_s, x_s, at_s, u_s, k_s, v_s,
    dq32, dqcat, own_scores, own_grads, sg_e, pr_e, sg_l, pr_l,
    acc_ke, acc_ve, acc_kl, acc_vl, ret_send, ret_recv,
    ri_buf, rg_buf, up_a, up_b, dn_a, dn_b,
    load_sem, kv_send, kv_recv, ret_sems, ri_sems, rg_sems,
    up_asem, up_bsem, dn_asem, dn_bsem, relay_sems,
):
    nd, nc, nh, half, group, rank = dims
    rows = 2 * half
    hq = half * group
    here_d, here_c, here_h = lax.axis_index("dp"), lax.axis_index("ctx"), lax.axis_index("head")
    is_shifted = here_h < nh // 2
    shifted = jnp.where(is_shifted, 1, 0)
    early = shifted * half
    late = (1 - shifted) * half
    early_q = pl.multiple_of(shifted * hq, hq)
    late_q = pl.multiple_of((1 - shifted) * hq, hq)
    early_m = pl.multiple_of(early, half)
    late_m = pl.multiple_of(late, half)
    after_c = lax.rem(here_c + 1, nc)
    before_c = lax.rem(here_c + nc - 1, nc)

    def in_head(step):
        return (here_d, here_c, lax.rem(here_h + step, nh))

    def in_ctx(step):
        return (here_d, lax.rem(here_c + step, nc), here_h)

    def in_dp(step):
        return (lax.rem(here_d + step, nd), here_c, here_h)

    flip = (here_d, here_c, here_h + 1 - 2 * lax.rem(here_h, 2))
    beside = [in_ctx(step) for step in sorted({1, nc - 1})]
    two_off = [in_ctx(step) for step in sorted({2, nc - 2}) if 0 < step < nc]
    near = (
        [flip]
        + [in_head(step) for step in sorted({2, 4, nh - 2}) if 0 < step < nh]
        + [in_dp(step) for step in range(nd - 1, 0, -1)]
        + beside
    )

    def tell(semaphore, peers):
        for peer in peers:
            pl.semaphore_signal(semaphore, inc=1, device_id=peer, device_id_type=MESH)

    barrier = pltpu.get_barrier_semaphore()
    tell(barrier, near)

    def local(src, dst, at):
        copy = pltpu.make_async_copy(src, dst, load_sem.at[at])
        copy.start()
        return copy

    load_ke = local(k_in.at[pl.ds(early_m, half)], k_s.at[pl.ds(0, half)], 0)
    load_ve = local(v_in.at[pl.ds(early_m, half)], v_s.at[pl.ds(0, half)], 1)
    load_qe = local(q_in.at[pl.ds(early_q, hq)], q_s.at[pl.ds(0, hq)], 2)
    load_de = local(do_in.at[pl.ds(early_q, hq)], do_s.at[pl.ds(0, hq)], 3)
    load_x = local(x_in, x_s, 5)
    load_at = local(at_in, at_s, 6)
    load_kl = local(k_in.at[pl.ds(late_m, half)], k_s.at[pl.ds(rows, half)], 7)
    load_vl = local(v_in.at[pl.ds(late_m, half)], v_s.at[pl.ds(rows, half)], 8)
    load_ql = local(q_in.at[pl.ds(late_q, hq)], q_s.at[pl.ds(hq, hq)], 9)
    load_dl = local(do_in.at[pl.ds(late_q, hq)], do_s.at[pl.ds(hq, hq)], 10)
    load_u = local(u_in, u_s, 11)

    def remote(src, dst, sends, recvs, peer):
        return pltpu.make_async_remote_copy(
            src_ref=src, dst_ref=dst, send_sem=sends, recv_sem=recvs, device_id=peer, device_id_type=MESH
        )

    def many(buf, count, sem):
        part = buf.at[pl.ds(0, count)]
        return pltpu.make_async_copy(part, part, sem)

    softmax_scale = 1.0 / math.sqrt(128)
    exp_scale = softmax_scale * math.log2(math.e)
    chunk = CHUNK
    per = chunk // group
    chunks = hq // chunk
    start_early = here_c * rows + early
    start_late = here_c * rows + late
    start_prev = jnp.where(is_shifted, before_c * rows + half, start_early)
    load_ke.wait()
    load_ve.wait()
    length = len_in[...]

    def own_part(at, keys, values, queries, live, base):
        key_at = lax.broadcasted_iota(jnp.int32, (half, chunk), 0)
        query_at = lax.broadcasted_iota(jnp.int32, (half, chunk), 1) // group + at * per
        allowed = (key_at <= query_at) & ((key_at < length - base) | (key_at == query_at))
        scores = jnp.where(allowed, mm(keys, queries, NT), BLOCKED)
        return scores, mm(values, live, NT)

    def finish(at, scores, prob_grad, keys, base, to, row0, grads_to, probs_to):
        top = jnp.max(scores, axis=0, keepdims=True)
        weights = jnp.exp2((scores - top) * exp_scale)
        total = jnp.sum(weights, axis=0, keepdims=True)
        query_row = lax.broadcasted_iota(jnp.int32, (1, chunk), 1) // group + at * per
        inverse = jnp.where(query_row < length - base, 1.0 / total, 0.0)
        probs = weights * inverse
        probs_low = probs.astype(BF16)
        out_dot = jnp.sum(probs_low.astype(F32) * prob_grad, axis=0, keepdims=True)
        score_grad = (probs * (prob_grad - out_dot)).astype(BF16)
        query_grad = mm(score_grad, keys, TN) * softmax_scale
        dq32[row0 + at * chunk : row0 + (at + 1) * chunk] = query_grad
        dq_out[pl.ds(pl.multiple_of(to + at * chunk, chunk), chunk), :] = query_grad.astype(BF16)
        lanes = slice(at * chunk, (at + 1) * chunk)
        grads_to[:, lanes] = score_grad
        probs_to[:, lanes] = probs_low

    def rank_part(row0, to):
        for g in range(group):
            dqcat[pl.ds(to, half), g * 128 : (g + 1) * 128] = dq32[pl.ds(row0 + g, half, stride=group), :].astype(
                BF16
            )
        rg_buf[here_h, :, pl.ds(to, half)] = mm(up_flat, dqcat[pl.ds(to, half), :], NT)

    pl.semaphore_wait(barrier, len(near))
    kv_copies = [
        remote(ref.at[pl.ds(0, half)], ref.at[pl.ds(half, half)], kv_send.at[at], kv_recv.at[at], in_ctx(1))
        for at, ref in enumerate((k_s, v_s))
    ]

    @pl.when(is_shifted)
    def _():
        for copy in kv_copies:
            copy.start()

    @pl.when(jnp.logical_not(is_shifted))
    def _():
        k_s[half:rows] = k_s[0:half]
        v_s[half:rows] = v_s[0:half]

    tell(relay_sems.at[0], [flip] + beside)

    load_qe.wait()
    load_de.wait()
    for at in range(chunks):
        place = slice(at * chunk, (at + 1) * chunk)
        keys = k_s[0:half]
        scores, prob_grad = own_part(at, keys, v_s[0:half], q_s[place], do_s[place], start_early)
        finish(at, scores, prob_grad, keys, start_early, early_q, 0, sg_e, pr_e)

    def head_exchange(buf, sems):
        for step in far_first(nh):
            remote(buf.at[here_h], buf.at[here_h], sems.at[0], sems.at[1], in_head(step)).start()

    load_x.wait()
    load_at.wait()
    ri_buf[here_h] = mm(at_s[...], x_s[...], NT)
    pl.semaphore_wait(relay_sems.at[0], 1 + len(beside))
    head_exchange(ri_buf, ri_sems)
    tell(relay_sems.at[1], two_off)

    load_kl.wait()
    load_vl.wait()
    load_ql.wait()
    load_dl.wait()
    for at in range(chunks):
        place = slice(hq + at * chunk, hq + (at + 1) * chunk)
        scores, prob_grad = own_part(
            at, k_s[rows : rows + half], v_s[rows : rows + half], q_s[place], do_s[place], start_late
        )
        own_scores[at] = scores
        own_grads[at] = prob_grad
    load_u.wait()
    up_flat = jnp.concatenate(
        [u_s[...].astype(F32).reshape(rank, group, 128)[:, g, :] for g in range(group)], axis=1
    ).astype(BF16)
    rank_part(0, early_m)
    acc_ke[...] = mm(sg_e[...], q_s[0:hq], NN)
    acc_ve[...] = mm(pr_e[...], do_s[0:hq], NN)

    @pl.when(is_shifted)
    def _():
        for copy in kv_copies:
            copy.wait()

    prev_seen = lax.broadcasted_iota(jnp.int32, (half, chunk), 0) < length - start_prev
    for at in range(chunks):
        place = slice(hq + at * chunk, hq + (at + 1) * chunk)
        prev_scores = jnp.where(prev_seen, mm(k_s[half:rows], q_s[place], NT), BLOCKED)
        scores = jnp.concatenate([prev_scores, own_scores[at]], axis=0)
        prob_grad = jnp.concatenate([mm(v_s[half:rows], do_s[place], NT), own_grads[at]], axis=0)
        finish(at, scores, prob_grad, k_s[half : rows + half], start_late, late_q, hq, sg_l, pr_l)

    rank_part(hq, late_m)
    head_exchange(rg_buf, rg_sems)
    acc_kl[...] = mm(sg_l[...], q_s[hq : 2 * hq], NN)
    acc_vl[...] = mm(pr_l[...], do_s[hq : 2 * hq], NN)

    ret_copy = remote(ret_send, ret_recv, ret_sems.at[0], ret_sems.at[1], in_ctx(nc - 1))

    @pl.when(is_shifted)
    def _():
        ret_send[0:half] = acc_kl[0:half].astype(BF16)
        ret_send[half:rows] = acc_vl[0:half].astype(BF16)
        ret_copy.start()

    wide = group * 128 // 2

    def send_over_dp(total, recv, sems):
        recv[here_d] = jnp.concatenate([total[:, :wide], total[:, wide:]], axis=0).astype(BF16)
        for step in range(nd - 1, 0, -1):
            remote(recv.at[here_d], recv.at[here_d], sems.at[0], sems.at[1], in_dp(step)).start()

    def send_over_ctx(recv, sems, onward, onward_sems):
        many(recv, nd - 1, sems.at[1]).wait()
        onward[here_c] = jnp.sum(recv[...].astype(F32), axis=0).astype(BF16)
        for step in far_first(nc):
            remote(
                onward.at[here_c], onward.at[here_c], onward_sems.at[0], onward_sems.at[1], in_ctx(step)
            ).start()

    def whole(recv, sems):
        many(recv, nc - 1, sems.at[1]).wait()
        total = jnp.sum(recv[...].astype(F32), axis=0)
        return jnp.concatenate([total[:rank], total[rank:]], axis=1)

    many(ri_buf, nh - 1, ri_sems.at[1]).wait()
    rank_input = jnp.sum(ri_buf[...], axis=0).astype(BF16)
    send_over_dp(mm(rank_input, dqcat[...], NN) * ADAPTER_SCALE, up_a, up_asem)

    dkv_out[0, pl.ds(late_m, half), :] = (acc_kl[half:rows] * softmax_scale).astype(BF16)
    dkv_out[1, pl.ds(late_m, half), :] = acc_vl[half:rows].astype(BF16)
    pl.semaphore_wait(relay_sems.at[1], len(two_off))
    send_over_ctx(up_a, up_asem, up_b, up_bsem)

    many(rg_buf, nh - 1, rg_sems.at[1]).wait()
    rank_grad = jnp.sum(rg_buf[...], axis=0).astype(BF16)
    send_over_dp(mm(rank_grad, x_s[...], NN) * ADAPTER_SCALE, dn_a, dn_asem)

    @pl.when(is_shifted)
    def _():
        ret_copy.wait()
        dkv_out[0, pl.ds(early_m, half), :] = (
            (acc_ke[...] + ret_recv[0:half].astype(F32)) * softmax_scale
        ).astype(BF16)
        dkv_out[1, pl.ds(early_m, half), :] = (acc_ve[...] + ret_recv[half:rows].astype(F32)).astype(BF16)

    @pl.when(jnp.logical_not(is_shifted))
    def _():
        dkv_out[0, pl.ds(early_m, half), :] = ((acc_ke[...] + acc_kl[0:half]) * softmax_scale).astype(BF16)
        dkv_out[1, pl.ds(early_m, half), :] = (acc_ve[...] + acc_vl[0:half]).astype(BF16)

    send_over_ctx(dn_a, dn_asem, dn_b, dn_bsem)
    up_whole = whole(up_b, up_bsem)
    for g in range(group):
        up_out[:, g, :] = up_whole[:, g * 128 : (g + 1) * 128]
    for buf, count, sem in (
        (ri_buf, nh - 1, ri_sems), (rg_buf, nh - 1, rg_sems), (up_a, nd - 1, up_asem),
        (dn_a, nd - 1, dn_asem), (up_b, nc - 1, up_bsem), (dn_b, nc - 1, dn_bsem),
    ):
        many(buf, count, sem.at[0]).wait()
    down_out[...] = whole(dn_b, dn_bsem)


def write_out(*refs):
    dq, dkv, down, up, dq_out, dk_out, dv_out, down_out, up_out, sems = refs
    pairs = ((dq, dq_out), (dkv.at[0], dk_out), (dkv.at[1], dv_out), (down, down_out), (up, up_out))
    copies = [pltpu.make_async_copy(src, dst, sems.at[at]) for at, (src, dst) in enumerate(pairs)]
    for copy in copies:
        copy.start()
    for copy in copies:
        copy.wait()


def on_device(sizes, q, k, v, do, x, adapter_down, adapter_up, lengths):
    nd, nc, nh = sizes
    rows, group, width = q.shape[1], q.shape[3], q.shape[4]
    rank, model = adapter_down.shape[1], x.shape[2]
    half = rows // 2
    hq = half * group
    dims = (nd, nc, nh, half, group, rank)
    hbm = pl.BlockSpec(memory_space=pltpu.HBM)
    vmem = pl.BlockSpec(memory_space=pltpu.VMEM)
    pair = pltpu.SemaphoreType.DMA((2,))
    packed = (2 * rank, group * width // 2)
    results = (
        ((rows * group, width), BF16),
        ((2, rows, width), BF16),
        ((rank, model), F32),
        ((rank, group, width), F32),
    )
    operands = (
        q.reshape(rows * group, width),
        k.reshape(rows, width),
        v.reshape(rows, width),
        do.reshape(rows * group, width),
        x.reshape(rows, model),
        adapter_down.T,
        adapter_up.reshape(rank * group, width),
    )
    made = pl.pallas_call(
        functools.partial(kernel, dims),
        out_shape=tuple(pltpu.VMEM(*one) for one in results),
        in_specs=[hbm] * 7 + [vmem],
        out_specs=(vmem,) * 4,
        scratch_shapes=[
            pltpu.VMEM((rows * group, width), BF16),
            pltpu.VMEM((rows * group, width), BF16),
            pltpu.VMEM((rows, model), BF16),
            pltpu.VMEM((rank, model), BF16),
            pltpu.VMEM((rank * group, width), BF16),
            pltpu.VMEM((rows + half, width), BF16),
            pltpu.VMEM((rows + half, width), BF16),
            pltpu.VMEM((rows * group, width), F32),
            pltpu.VMEM((rows, group * width), BF16),
            pltpu.VMEM((hq // CHUNK, half, CHUNK), F32),
            pltpu.VMEM((hq // CHUNK, half, CHUNK), F32),
            pltpu.VMEM((half, hq), BF16),
            pltpu.VMEM((half, hq), BF16),
            pltpu.VMEM((rows, hq), BF16),
            pltpu.VMEM((rows, hq), BF16),
            pltpu.VMEM((half, width), F32),
            pltpu.VMEM((half, width), F32),
            pltpu.VMEM((rows, width), F32),
            pltpu.VMEM((rows, width), F32),
            pltpu.VMEM((rows, width), BF16),
            pltpu.VMEM((rows, width), BF16),
            pltpu.VMEM((nh, rank, rows), F32),
            pltpu.VMEM((nh, rank, rows), F32),
        ]
        + [
            pltpu.VMEM((nd,) + packed, BF16),
            pltpu.VMEM((nc,) + packed, BF16),
        ]
        * 2
        + [pltpu.SemaphoreType.DMA((12,))]
        + [pair] * 9
        + [pltpu.SemaphoreType.REGULAR((2,))],
        compiler_params=pltpu.CompilerParams(
            collective_id=0, has_side_effects=True, vmem_limit_bytes=40 * 1024 * 1024
        ),
        name="attention_and_rank_gradients",
    )(
        *(pltpu.with_memory_space_constraint(one, pltpu.HBM) for one in operands),
        pltpu.with_memory_space_constraint(jnp.broadcast_to(lengths[:, None], (1, CHUNK)), pltpu.VMEM),
    )
    dq, dk, dv, down, up = pl.pallas_call(
        write_out,
        out_shape=(
            jax.ShapeDtypeStruct(*results[0]),
            jax.ShapeDtypeStruct((rows, width), BF16),
            jax.ShapeDtypeStruct((rows, width), BF16),
            jax.ShapeDtypeStruct(*results[2]),
            jax.ShapeDtypeStruct(*results[3]),
        ),
        in_specs=[vmem] * 4,
        out_specs=(hbm,) * 5,
        scratch_shapes=[pltpu.SemaphoreType.DMA((5,))],
        name="write_results",
    )(*(pltpu.with_memory_space_constraint(one, pltpu.VMEM) for one in made))
    return (
        dq.reshape(q.shape),
        dk.reshape(k.shape),
        dv.reshape(v.shape),
        down.T,
        up.reshape(adapter_up.shape),
    )


def solution(mesh):
    sizes = (mesh.shape["dp"], mesh.shape["ctx"], mesh.shape["head"])
    return jax.shard_map(
        functools.partial(on_device, sizes),
        mesh=mesh,
        in_specs=(
            P("dp", "ctx", "head", None, None),
            P("dp", "ctx", "head", None),
            P("dp", "ctx", "head", None),
            P("dp", "ctx", "head", None, None),
            P("dp", "ctx", "head"),
            P("head", None),
            P(None, "head", None, None),
            P("dp"),
        ),
        out_specs=(
            P("dp", "ctx", "head", None, None),
            P("dp", "ctx", "head", None),
            P("dp", "ctx", "head", None),
            P("head", None),
            P(None, "head", None, None),
        ),
        check_vma=False,
    )
```

```python
import functools
import math

import jax
import jax.numpy as jnp
from jax import lax
from jax.experimental import pallas as pl
from jax.experimental.pallas import tpu as pltpu
from jax.sharding import PartitionSpec as P

ADAPTER_SCALE = 2.0
BLOCKED = -1e30
CHUNK = 512
MESH = pl.DeviceIdType.MESH
F32 = jnp.float32
BF16 = jnp.bfloat16
NT = (((1,), (1,)), ((), ()))
NN = (((1,), (0,)), ((), ()))
TN = (((0,), (0,)), ((), ()))


def far_first(count):
    return sorted(range(1, count), key=lambda step: -min(step, count - step))


def mm(a, b, dims):
    return lax.dot_general(a, b, dims, preferred_element_type=F32)


def kernel(
    dims,
    q_in, k_in, v_in, do_in, x_in, at_in, u_in, len_in,
    dq_out, dkv_out, down_out, up_out,
    q_s, do_s, x_s, at_s, u_s, k_s, v_s,
    dq32, dqcat, own_scores, own_grads, sg_e, pr_e, sg_l, pr_l,
    acc_ke, acc_ve, acc_kl, acc_vl, ret_send, ret_recv,
    ri_buf, rg_buf, up_p, up_a, up_b, up_c, dn_a, dn_b,
    load_sem, kv_send, kv_recv, ret_sems, ri_sems, rg_sems,
    up_asem, up_bsem, up_csem, dn_asem, dn_bsem, relay_sems,
):
    nd, nc, nh, half, group, rank = dims
    rows = 2 * half
    hq = half * group
    here_d, here_c, here_h = lax.axis_index("dp"), lax.axis_index("ctx"), lax.axis_index("head")
    is_shifted = here_h < nh // 2
    core = lax.rem(here_d, 2)
    shifted = jnp.where(is_shifted, 1, 0)
    early = shifted * half
    late = (1 - shifted) * half
    early_q = pl.multiple_of(shifted * hq, hq)
    late_q = pl.multiple_of((1 - shifted) * hq, hq)
    early_m = pl.multiple_of(early, half)
    late_m = pl.multiple_of(late, half)
    after_c = lax.rem(here_c + 1, nc)
    before_c = lax.rem(here_c + nc - 1, nc)

    def in_head(step):
        return (here_d, here_c, lax.rem(here_h + step, nh))

    def in_ctx(step):
        return (here_d, lax.rem(here_c + step, nc), here_h)

    def in_dp(step):
        return (lax.rem(here_d + step, nd), here_c, here_h)

    flip = (here_d, here_c, here_h + 1 - 2 * lax.rem(here_h, 2))
    beside = [in_ctx(step) for step in sorted({1, nc - 1})]
    two_off = [in_ctx(step) for step in sorted({2, nc - 2}) if 0 < step < nc]
    near = (
        [flip]
        + [in_head(step) for step in sorted({2, 4, nh - 2}) if 0 < step < nh]
        + [in_dp(step) for step in range(nd - 1, 0, -1)]
        + beside
    )

    def tell(semaphore, peers):
        for peer in peers:
            pl.semaphore_signal(semaphore, inc=1, device_id=peer, device_id_type=MESH)

    barrier = pltpu.get_barrier_semaphore()
    tell(barrier, near)

    def local(src, dst, at):
        copy = pltpu.make_async_copy(src, dst, load_sem.at[at])
        copy.start()
        return copy

    load_ke = local(k_in.at[pl.ds(early_m, half)], k_s.at[pl.ds(0, half)], 0)
    load_ve = local(v_in.at[pl.ds(early_m, half)], v_s.at[pl.ds(0, half)], 1)
    load_qe = local(q_in.at[pl.ds(early_q, hq)], q_s.at[pl.ds(0, hq)], 2)
    load_de = local(do_in.at[pl.ds(early_q, hq)], do_s.at[pl.ds(0, hq)], 3)
    load_x = local(x_in, x_s, 5)
    load_at = local(at_in, at_s, 6)
    load_kl = local(k_in.at[pl.ds(late_m, half)], k_s.at[pl.ds(rows, half)], 7)
    load_vl = local(v_in.at[pl.ds(late_m, half)], v_s.at[pl.ds(rows, half)], 8)
    load_ql = local(q_in.at[pl.ds(late_q, hq)], q_s.at[pl.ds(hq, hq)], 9)
    load_dl = local(do_in.at[pl.ds(late_q, hq)], do_s.at[pl.ds(hq, hq)], 10)
    load_u = local(u_in, u_s, 11)

    def remote(src, dst, sends, recvs, peer):
        return pltpu.make_async_remote_copy(
            src_ref=src, dst_ref=dst, send_sem=sends, recv_sem=recvs, device_id=peer, device_id_type=MESH
        )

    def many(buf, count, sem):
        part = buf.at[pl.ds(0, count)]
        return pltpu.make_async_copy(part, part, sem)

    softmax_scale = 1.0 / math.sqrt(128)
    exp_scale = softmax_scale * math.log2(math.e)
    chunk = CHUNK
    per = chunk // group
    chunks = hq // chunk
    start_early = here_c * rows + early
    start_late = here_c * rows + late
    start_prev = jnp.where(is_shifted, before_c * rows + half, start_early)
    load_ke.wait()
    load_ve.wait()
    length = len_in[...]

    def own_part(at, keys, values, queries, live, base):
        key_at = lax.broadcasted_iota(jnp.int32, (half, chunk), 0)
        query_at = lax.broadcasted_iota(jnp.int32, (half, chunk), 1) // group + at * per
        allowed = (key_at <= query_at) & ((key_at < length - base) | (key_at == query_at))
        scores = jnp.where(allowed, mm(keys, queries, NT), BLOCKED)
        return scores, mm(values, live, NT)

    def finish(at, scores, prob_grad, keys, base, to, row0, grads_to, probs_to):
        top = jnp.max(scores, axis=0, keepdims=True)
        weights = jnp.exp2((scores - top) * exp_scale)
        total = jnp.sum(weights, axis=0, keepdims=True)
        query_row = lax.broadcasted_iota(jnp.int32, (1, chunk), 1) // group + at * per
        inverse = jnp.where(query_row < length - base, 1.0 / total, 0.0)
        probs = weights * inverse
        probs_low = probs.astype(BF16)
        out_dot = jnp.sum(probs_low.astype(F32) * prob_grad, axis=0, keepdims=True)
        score_grad = (probs * (prob_grad - out_dot)).astype(BF16)
        query_grad = mm(score_grad, keys, TN) * softmax_scale
        dq32[row0 + at * chunk : row0 + (at + 1) * chunk] = query_grad
        dq_out[pl.ds(pl.multiple_of(to + at * chunk, chunk), chunk), :] = query_grad.astype(BF16)
        lanes = slice(at * chunk, (at + 1) * chunk)
        grads_to[:, lanes] = score_grad
        probs_to[:, lanes] = probs_low

    def rank_part(row0, to):
        for g in range(group):
            dqcat[pl.ds(to, half), g * 128 : (g + 1) * 128] = dq32[pl.ds(row0 + g, half, stride=group), :].astype(
                BF16
            )
        rg_buf[here_h, :, pl.ds(to, half)] = mm(up_flat, dqcat[pl.ds(to, half), :], NT)

    pl.semaphore_wait(barrier, len(near))
    kv_copies = [
        remote(ref.at[pl.ds(0, half)], ref.at[pl.ds(half, half)], kv_send.at[at], kv_recv.at[at], in_ctx(1))
        for at, ref in enumerate((k_s, v_s))
    ]

    @pl.when(is_shifted)
    def _():
        for copy in kv_copies:
            copy.start()

    @pl.when(jnp.logical_not(is_shifted))
    def _():
        k_s[half:rows] = k_s[0:half]
        v_s[half:rows] = v_s[0:half]

    tell(relay_sems.at[0], [flip] + beside)

    load_qe.wait()
    load_de.wait()
    for at in range(chunks):
        place = slice(at * chunk, (at + 1) * chunk)
        keys = k_s[0:half]
        scores, prob_grad = own_part(at, keys, v_s[0:half], q_s[place], do_s[place], start_early)
        finish(at, scores, prob_grad, keys, start_early, early_q, 0, sg_e, pr_e)

    def head_exchange(buf, sems):
        for step in far_first(nh):
            remote(buf.at[here_h], buf.at[here_h], sems.at[0], sems.at[1], in_head(step)).start()

    load_x.wait()
    load_at.wait()
    ri_buf[here_h] = mm(at_s[...], x_s[...], NT)
    load_kl.wait()
    load_vl.wait()
    load_ql.wait()
    load_dl.wait()
    for at in range(chunks):
        place = slice(hq + at * chunk, hq + (at + 1) * chunk)
        scores, prob_grad = own_part(
            at, k_s[rows : rows + half], v_s[rows : rows + half], q_s[place], do_s[place], start_late
        )
        own_scores[at] = scores
        own_grads[at] = prob_grad
    load_u.wait()
    up_flat = jnp.concatenate(
        [u_s[...].astype(F32).reshape(rank, group, 128)[:, g, :] for g in range(group)], axis=1
    ).astype(BF16)
    rank_part(0, early_m)
    acc_ke[...] = mm(sg_e[...], q_s[0:hq], NN)
    acc_ve[...] = mm(pr_e[...], do_s[0:hq], NN)
    pl.semaphore_wait(relay_sems.at[0], 1 + len(beside))
    head_exchange(ri_buf, ri_sems)
    tell(relay_sems.at[1], two_off)


    @pl.when(is_shifted)
    def _():
        for copy in kv_copies:
            copy.wait()

    prev_seen = lax.broadcasted_iota(jnp.int32, (half, chunk), 0) < length - start_prev
    for at in range(chunks):
        place = slice(hq + at * chunk, hq + (at + 1) * chunk)
        prev_scores = jnp.where(prev_seen, mm(k_s[half:rows], q_s[place], NT), BLOCKED)
        scores = jnp.concatenate([prev_scores, own_scores[at]], axis=0)
        prob_grad = jnp.concatenate([mm(v_s[half:rows], do_s[place], NT), own_grads[at]], axis=0)
        finish(at, scores, prob_grad, k_s[half : rows + half], start_late, late_q, hq, sg_l, pr_l)

    rank_part(hq, late_m)
    head_exchange(rg_buf, rg_sems)
    acc_kl[...] = mm(sg_l[...], q_s[hq : 2 * hq], NN)
    acc_vl[...] = mm(pr_l[...], do_s[hq : 2 * hq], NN)

    ret_copy = remote(ret_send, ret_recv, ret_sems.at[0], ret_sems.at[1], in_ctx(nc - 1))

    @pl.when(is_shifted)
    def _():
        ret_send[0:half] = acc_kl[0:half].astype(BF16)
        ret_send[half:rows] = acc_vl[0:half].astype(BF16)
        ret_copy.start()

    wide = group * 128 // 2

    def send_over_dp(total, recv, sems):
        recv[here_d] = jnp.concatenate([total[:, :wide], total[:, wide:]], axis=0).astype(BF16)
        for step in range(nd - 1, 0, -1):
            remote(recv.at[here_d], recv.at[here_d], sems.at[0], sems.at[1], in_dp(step)).start()

    def send_over_ctx(recv, sems, onward, onward_sems):
        many(recv, nd - 1, sems.at[1]).wait()
        onward[here_c] = jnp.sum(recv[...].astype(F32), axis=0).astype(BF16)
        for step in far_first(nc):
            remote(
                onward.at[here_c], onward.at[here_c], onward_sems.at[0], onward_sems.at[1], in_ctx(step)
            ).start()

    def send_halves_over_dp(total, part, recv, sems):
        for at in range(2):
            left = at * wide
            part[at] = jnp.concatenate(
                [total[:, left : left + wide // 2], total[:, left + wide // 2 : left + wide]], axis=0
            ).astype(BF16)
        recv[here_d] = part[core]
        for step in range(nd - 1, 0, -1):
            peer = in_dp(step)
            remote(part.at[lax.rem(peer[0], 2)], recv.at[here_d], sems.at[0], sems.at[1], peer).start()

    def swap_halves(recv, sems, both, both_sems):
        many(recv, nc - 1, sems.at[1]).wait()
        both[core] = jnp.sum(recv[...].astype(F32), axis=0)
        copy = remote(
            both.at[core], both.at[core], both_sems.at[0], both_sems.at[1], (here_d + 1 - 2 * core, here_c, here_h)
        )
        copy.start()
        return copy

    def whole(recv, sems):
        many(recv, nc - 1, sems.at[1]).wait()
        total = jnp.sum(recv[...].astype(F32), axis=0)
        return jnp.concatenate([total[:rank], total[rank:]], axis=1)

    many(ri_buf, nh - 1, ri_sems.at[1]).wait()
    rank_input = jnp.sum(ri_buf[...], axis=0).astype(BF16)
    send_halves_over_dp(mm(rank_input, dqcat[...], NN) * ADAPTER_SCALE, up_p, up_a, up_asem)

    many(rg_buf, nh - 1, rg_sems.at[1]).wait()
    rank_grad = jnp.sum(rg_buf[...], axis=0).astype(BF16)
    send_over_dp(mm(rank_grad, x_s[...], NN) * ADAPTER_SCALE, dn_a, dn_asem)

    pl.semaphore_wait(relay_sems.at[1], len(two_off))
    send_over_ctx(up_a, up_asem, up_b, up_bsem)

    dkv_out[0, pl.ds(late_m, half), :] = (acc_kl[half:rows] * softmax_scale).astype(BF16)
    dkv_out[1, pl.ds(late_m, half), :] = acc_vl[half:rows].astype(BF16)

    @pl.when(is_shifted)
    def _():
        ret_copy.wait()
        dkv_out[0, pl.ds(early_m, half), :] = (
            (acc_ke[...] + ret_recv[0:half].astype(F32)) * softmax_scale
        ).astype(BF16)
        dkv_out[1, pl.ds(early_m, half), :] = (acc_ve[...] + ret_recv[half:rows].astype(F32)).astype(BF16)

    @pl.when(jnp.logical_not(is_shifted))
    def _():
        dkv_out[0, pl.ds(early_m, half), :] = ((acc_ke[...] + acc_kl[0:half]) * softmax_scale).astype(BF16)
        dkv_out[1, pl.ds(early_m, half), :] = (acc_ve[...] + acc_vl[0:half]).astype(BF16)

    send_over_ctx(dn_a, dn_asem, dn_b, dn_bsem)
    up_swap = swap_halves(up_b, up_bsem, up_c, up_csem)
    up_swap.wait()
    up_whole = jnp.concatenate(
        [up_c[at, rank * row : rank * (row + 1)] for at in range(2) for row in range(2)], axis=1
    )
    for g in range(group):
        up_out[:, g, :] = up_whole[:, g * 128 : (g + 1) * 128]
    for buf, count, sem in (
        (ri_buf, nh - 1, ri_sems), (rg_buf, nh - 1, rg_sems), (up_a, nd - 1, up_asem),
        (dn_a, nd - 1, dn_asem), (up_b, nc - 1, up_bsem), (dn_b, nc - 1, dn_bsem),
    ):
        many(buf, count, sem.at[0]).wait()
    down_out[...] = whole(dn_b, dn_bsem)


def write_out(*refs):
    dq, dkv, down, up, dq_out, dk_out, dv_out, down_out, up_out, sems = refs
    pairs = ((dq, dq_out), (dkv.at[0], dk_out), (dkv.at[1], dv_out), (down, down_out), (up, up_out))
    copies = [pltpu.make_async_copy(src, dst, sems.at[at]) for at, (src, dst) in enumerate(pairs)]
    for copy in copies:
        copy.start()
    for copy in copies:
        copy.wait()


def on_device(sizes, q, k, v, do, x, adapter_down, adapter_up, lengths):
    nd, nc, nh = sizes
    rows, group, width = q.shape[1], q.shape[3], q.shape[4]
    rank, model = adapter_down.shape[1], x.shape[2]
    half = rows // 2
    hq = half * group
    dims = (nd, nc, nh, half, group, rank)
    hbm = pl.BlockSpec(memory_space=pltpu.HBM)
    vmem = pl.BlockSpec(memory_space=pltpu.VMEM)
    pair = pltpu.SemaphoreType.DMA((2,))
    packed = (2 * rank, group * width // 2)
    halved = (2 * rank, group * width // 4)
    results = (
        ((rows * group, width), BF16),
        ((2, rows, width), BF16),
        ((rank, model), F32),
        ((rank, group, width), F32),
    )
    operands = (
        q.reshape(rows * group, width),
        k.reshape(rows, width),
        v.reshape(rows, width),
        do.reshape(rows * group, width),
        x.reshape(rows, model),
        adapter_down.T,
        adapter_up.reshape(rank * group, width),
    )
    made = pl.pallas_call(
        functools.partial(kernel, dims),
        out_shape=tuple(pltpu.VMEM(*one) for one in results),
        in_specs=[hbm] * 7 + [vmem],
        out_specs=(vmem,) * 4,
        scratch_shapes=[
            pltpu.VMEM((rows * group, width), BF16),
            pltpu.VMEM((rows * group, width), BF16),
            pltpu.VMEM((rows, model), BF16),
            pltpu.VMEM((rank, model), BF16),
            pltpu.VMEM((rank * group, width), BF16),
            pltpu.VMEM((rows + half, width), BF16),
            pltpu.VMEM((rows + half, width), BF16),
            pltpu.VMEM((rows * group, width), F32),
            pltpu.VMEM((rows, group * width), BF16),
            pltpu.VMEM((hq // CHUNK, half, CHUNK), F32),
            pltpu.VMEM((hq // CHUNK, half, CHUNK), F32),
            pltpu.VMEM((half, hq), BF16),
            pltpu.VMEM((half, hq), BF16),
            pltpu.VMEM((rows, hq), BF16),
            pltpu.VMEM((rows, hq), BF16),
            pltpu.VMEM((half, width), F32),
            pltpu.VMEM((half, width), F32),
            pltpu.VMEM((rows, width), F32),
            pltpu.VMEM((rows, width), F32),
            pltpu.VMEM((rows, width), BF16),
            pltpu.VMEM((rows, width), BF16),
            pltpu.VMEM((nh, rank, rows), F32),
            pltpu.VMEM((nh, rank, rows), F32),
        ]
        + [
            pltpu.VMEM((2,) + halved, BF16),
            pltpu.VMEM((nd,) + halved, BF16),
            pltpu.VMEM((nc,) + halved, BF16),
            pltpu.VMEM((2,) + halved, F32),
            pltpu.VMEM((nd,) + packed, BF16),
            pltpu.VMEM((nc,) + packed, BF16),
        ]
        + [pltpu.SemaphoreType.DMA((12,))]
        + [pair] * 10
        + [pltpu.SemaphoreType.REGULAR((2,))],
        compiler_params=pltpu.CompilerParams(
            collective_id=0, has_side_effects=True, vmem_limit_bytes=40 * 1024 * 1024
        ),
        name="attention_and_rank_gradients",
    )(
        *(pltpu.with_memory_space_constraint(one, pltpu.HBM) for one in operands),
        pltpu.with_memory_space_constraint(jnp.broadcast_to(lengths[:, None], (1, CHUNK)), pltpu.VMEM),
    )
    dq, dk, dv, down, up = pl.pallas_call(
        write_out,
        out_shape=(
            jax.ShapeDtypeStruct(*results[0]),
            jax.ShapeDtypeStruct((rows, width), BF16),
            jax.ShapeDtypeStruct((rows, width), BF16),
            jax.ShapeDtypeStruct(*results[2]),
            jax.ShapeDtypeStruct(*results[3]),
        ),
        in_specs=[vmem] * 4,
        out_specs=(hbm,) * 5,
        scratch_shapes=[pltpu.SemaphoreType.DMA((5,))],
        name="write_results",
    )(*(pltpu.with_memory_space_constraint(one, pltpu.VMEM) for one in made))
    return (
        dq.reshape(q.shape),
        dk.reshape(k.shape),
        dv.reshape(v.shape),
        down.T,
        up.reshape(adapter_up.shape),
    )


def solution(mesh):
    sizes = (mesh.shape["dp"], mesh.shape["ctx"], mesh.shape["head"])
    return jax.shard_map(
        functools.partial(on_device, sizes),
        mesh=mesh,
        in_specs=(
            P("dp", "ctx", "head", None, None),
            P("dp", "ctx", "head", None),
            P("dp", "ctx", "head", None),
            P("dp", "ctx", "head", None, None),
            P("dp", "ctx", "head"),
            P("head", None),
            P(None, "head", None, None),
            P("dp"),
        ),
        out_specs=(
            P("dp", "ctx", "head", None, None),
            P("dp", "ctx", "head", None),
            P("dp", "ctx", "head", None),
            P("head", None),
            P(None, "head", None, None),
        ),
        check_vma=False,
    )
```

```python
import functools
import math

import jax
import jax.numpy as jnp
from jax import lax
from jax.experimental import pallas as pl
from jax.experimental.pallas import tpu as pltpu
from jax.sharding import PartitionSpec as P

ADAPTER_SCALE = 2.0
BLOCKED = -1e30
CHUNK = 1024
MESH = pl.DeviceIdType.MESH
F32 = jnp.float32
BF16 = jnp.bfloat16
NT = (((1,), (1,)), ((), ()))
NN = (((1,), (0,)), ((), ()))
TN = (((0,), (0,)), ((), ()))


def far_first(count):
    return sorted(range(1, count), key=lambda step: -min(step, count - step))


def mm(a, b, dims):
    return lax.dot_general(a, b, dims, preferred_element_type=F32)


def kernel(
    dims,
    q_in, k_in, v_in, do_in, x_in, at_in, u_in, len_in,
    dq_out, dkv_out, down_out, up_out,
    q_s, do_s, x_s, at_s, u_s, k_s, v_s,
    dq32, dqcat, own_scores, own_grads, sg_e, pr_e, sg_l, pr_l, fold,
    acc_ke, acc_ve, acc_kl, acc_vl, ret_send, ret_recv,
    ri_buf, rg_buf, up_p, up_a, up_b, up_c, dn_a, dn_b,
    load_sem, kv_send, kv_recv, ret_sems, ri_sems, rg_sems,
    up_asem, up_bsem, up_csem, dn_asem, dn_bsem, relay_sems,
):
    nd, nc, nh, half, group, rank = dims
    rows = 2 * half
    hq = half * group
    here_d, here_c, here_h = lax.axis_index("dp"), lax.axis_index("ctx"), lax.axis_index("head")
    is_shifted = here_h < nh // 2
    core = lax.rem(here_d, 2)
    shifted = jnp.where(is_shifted, 1, 0)
    early = shifted * half
    late = (1 - shifted) * half
    early_q = pl.multiple_of(shifted * hq, hq)
    late_q = pl.multiple_of((1 - shifted) * hq, hq)
    early_m = pl.multiple_of(early, half)
    late_m = pl.multiple_of(late, half)
    after_c = lax.rem(here_c + 1, nc)
    before_c = lax.rem(here_c + nc - 1, nc)

    def in_head(step):
        return (here_d, here_c, lax.rem(here_h + step, nh))

    def in_ctx(step):
        return (here_d, lax.rem(here_c + step, nc), here_h)

    def dp_peers():
        moves = [(x, c) for x in range(nd // 2 - 1, -1, -1) for c in (1, 0) if (x, c) != (0, 0)]
        return [
            (lax.rem(here_d // 2 + x, nd // 2) * 2 + lax.rem(core + c, 2), here_c, here_h) for x, c in moves
        ]

    def head_peers():
        ny, side = nh // 2, lax.rem(here_h, 2)
        moves = [(y, x) for y in range(ny) for x in range(2) if (y, x) != (0, 0)]
        moves.sort(key=lambda move: -(min(move[0], ny - move[0]) + 2 * move[1]))
        return [
            (here_d, here_c, lax.rem(here_h // 2 + y, ny) * 2 + lax.rem(side + x, 2)) for y, x in moves
        ]

    flip = (here_d, here_c, here_h + 1 - 2 * lax.rem(here_h, 2))
    beside = [in_ctx(step) for step in sorted({1, nc - 1})]
    two_off = [in_ctx(step) for step in sorted({2, nc - 2}) if 0 < step < nc]
    near = (
        [flip]
        + [in_head(step) for step in sorted({2, 4, nh - 2}) if 0 < step < nh]
        + dp_peers()
        + beside
    )

    def tell(semaphore, peers):
        for peer in peers:
            pl.semaphore_signal(semaphore, inc=1, device_id=peer, device_id_type=MESH)

    barrier = pltpu.get_barrier_semaphore()
    tell(barrier, near)

    def local(src, dst, at):
        copy = pltpu.make_async_copy(src, dst, load_sem.at[at])
        copy.start()
        return copy

    load_ke = local(k_in.at[pl.ds(early_m, half)], k_s.at[pl.ds(0, half)], 0)
    load_ve = local(v_in.at[pl.ds(early_m, half)], v_s.at[pl.ds(0, half)], 1)
    load_qe = local(q_in.at[pl.ds(early_q, hq)], q_s.at[pl.ds(0, hq)], 2)
    load_de = local(do_in.at[pl.ds(early_q, hq)], do_s.at[pl.ds(0, hq)], 3)
    load_x = local(x_in, x_s, 5)
    load_at = local(at_in, at_s, 6)
    load_kl = local(k_in.at[pl.ds(late_m, half)], k_s.at[pl.ds(rows, half)], 7)
    load_vl = local(v_in.at[pl.ds(late_m, half)], v_s.at[pl.ds(rows, half)], 8)
    load_ql = local(q_in.at[pl.ds(late_q, hq)], q_s.at[pl.ds(hq, hq)], 9)
    load_dl = local(do_in.at[pl.ds(late_q, hq)], do_s.at[pl.ds(hq, hq)], 10)
    load_u = local(u_in, u_s, 11)

    def remote(src, dst, sends, recvs, peer):
        return pltpu.make_async_remote_copy(
            src_ref=src, dst_ref=dst, send_sem=sends, recv_sem=recvs, device_id=peer, device_id_type=MESH
        )

    def many(buf, count, sem):
        part = buf.at[pl.ds(0, count)]
        return pltpu.make_async_copy(part, part, sem)

    softmax_scale = 1.0 / math.sqrt(128)
    exp_scale = softmax_scale * math.log2(math.e)
    chunk = CHUNK
    per = chunk // group
    chunks = hq // chunk
    start_early = here_c * rows + early
    start_late = here_c * rows + late
    start_prev = jnp.where(is_shifted, before_c * rows + half, start_early)
    load_ke.wait()
    load_ve.wait()
    length = len_in[...]

    def own_part(at, keys, values, queries, live, base):
        key_at = lax.broadcasted_iota(jnp.int32, (half, chunk), 0)
        query_at = lax.broadcasted_iota(jnp.int32, (half, chunk), 1) // group + at * per
        allowed = (key_at <= query_at) & ((key_at < length - base) | (key_at == query_at))
        scores = jnp.where(allowed, mm(keys, queries, NT), BLOCKED)
        return scores, mm(values, live, NT)

    def finish(at, scores, prob_grad, base, grads_to, probs_to):
        top = jnp.max(scores, axis=0, keepdims=True)
        weights = jnp.exp2((scores - top) * exp_scale)
        total = jnp.sum(weights, axis=0, keepdims=True)
        query_row = lax.broadcasted_iota(jnp.int32, (1, chunk), 1) // group + at * per
        inverse = jnp.where(query_row < length - base, 1.0 / total, 0.0)
        probs = weights * inverse
        probs_low = probs.astype(BF16)
        out_dot = jnp.sum(probs_low.astype(F32) * prob_grad, axis=0, keepdims=True)
        score_grad = (probs * (prob_grad - out_dot)).astype(BF16)
        lanes = slice(at * chunk, (at + 1) * chunk)
        grads_to[:, lanes] = score_grad
        probs_to[:, lanes] = probs_low
        return score_grad

    def query_part(at, score_grad, keys, to, row0):
        query_grad = mm(score_grad, keys, TN) * softmax_scale
        dq32[row0 + at * chunk : row0 + (at + 1) * chunk] = query_grad
        dq_out[pl.ds(pl.multiple_of(to + at * chunk, chunk), chunk), :] = query_grad.astype(BF16)

    def by_head(row0, to):
        for g in range(group):
            dqcat[pl.ds(to, half), g * 128 : (g + 1) * 128] = dq32[pl.ds(row0 + g, half, stride=group), :].astype(
                BF16
            )

    pl.semaphore_wait(barrier, len(near))
    kv_copies = [
        remote(ref.at[pl.ds(0, half)], ref.at[pl.ds(half, half)], kv_send.at[at], kv_recv.at[at], in_ctx(1))
        for at, ref in enumerate((k_s, v_s))
    ]

    @pl.when(is_shifted)
    def _():
        for copy in kv_copies:
            copy.start()

    @pl.when(jnp.logical_not(is_shifted))
    def _():
        k_s[half:rows] = k_s[0:half]
        v_s[half:rows] = v_s[0:half]

    tell(relay_sems.at[0], [flip] + beside)

    load_qe.wait()
    load_de.wait()
    for at in range(chunks):
        place = slice(at * chunk, (at + 1) * chunk)
        keys = k_s[0:half]
        scores, prob_grad = own_part(at, keys, v_s[0:half], q_s[place], do_s[place], start_early)
        query_part(at, finish(at, scores, prob_grad, start_early, sg_e, pr_e), keys, early_q, 0)

    def head_exchange(buf, sems):
        for peer in head_peers():
            remote(buf.at[here_h], buf.at[here_h], sems.at[0], sems.at[1], peer).start()

    load_x.wait()
    load_at.wait()
    ri_buf[here_h] = mm(at_s[...], x_s[...], NT)
    load_kl.wait()
    load_vl.wait()
    load_ql.wait()
    load_dl.wait()
    for at in range(chunks):
        place = slice(hq + at * chunk, hq + (at + 1) * chunk)
        scores, prob_grad = own_part(
            at, k_s[rows : rows + half], v_s[rows : rows + half], q_s[place], do_s[place], start_late
        )
        own_scores[at] = scores
        own_grads[at] = prob_grad
    load_u.wait()
    up_heads = [u_s[...].astype(F32).reshape(rank, group, 128)[:, g, :] for g in range(group)]
    up_flat = jnp.concatenate(up_heads, axis=1).astype(BF16)
    up_tall = jnp.concatenate(up_heads, axis=0).astype(BF16)
    by_head(0, early_m)
    rg_buf[here_h, :, pl.ds(early_m, half)] = mm(up_flat, dqcat[pl.ds(early_m, half), :], NT)
    fold[...] = jnp.where(
        lax.broadcasted_iota(jnp.int32, (hq, half), 0) // group == lax.broadcasted_iota(jnp.int32, (hq, half), 1),
        1.0,
        0.0,
    ).astype(BF16)
    acc_ke[...] = mm(sg_e[...], q_s[0:hq], NN)
    acc_ve[...] = mm(pr_e[...], do_s[0:hq], NN)
    pl.semaphore_wait(relay_sems.at[0], 1 + len(beside))
    head_exchange(ri_buf, ri_sems)
    tell(relay_sems.at[1], two_off)


    @pl.when(is_shifted)
    def _():
        for copy in kv_copies:
            copy.wait()

    key_up = (mm(up_tall, k_s[half : rows + half], NT) * softmax_scale).astype(BF16)
    lane_head = lax.rem(lax.broadcasted_iota(jnp.int32, (rank, chunk), 1), group)
    prev_seen = lax.broadcasted_iota(jnp.int32, (half, chunk), 0) < length - start_prev
    folded = []
    for at in range(chunks):
        place = slice(hq + at * chunk, hq + (at + 1) * chunk)
        prev_scores = jnp.where(prev_seen, mm(k_s[half:rows], q_s[place], NT), BLOCKED)
        scores = jnp.concatenate([prev_scores, own_scores[at]], axis=0)
        prob_grad = jnp.concatenate([mm(v_s[half:rows], do_s[place], NT), own_grads[at]], axis=0)
        all_heads = mm(key_up, finish(at, scores, prob_grad, start_late, sg_l, pr_l), NN)
        own_head = jnp.zeros((rank, chunk), F32)
        for g in range(group):
            own_head += jnp.where(lane_head == g, all_heads[rank * g : rank * (g + 1)], 0.0)
        rest = own_head - own_head.astype(BF16).astype(F32)
        both = jnp.concatenate([own_head, rest], axis=0).astype(BF16)
        folded.append(mm(both, fold[at * chunk : (at + 1) * chunk], NN))

    folded = sum(folded)
    rg_buf[here_h, :, pl.ds(late_m, half)] = folded[:rank] + folded[rank:]
    head_exchange(rg_buf, rg_sems)
    for at in range(chunks):
        query_part(at, sg_l[:, at * chunk : (at + 1) * chunk], k_s[half : rows + half], late_q, hq)
    by_head(hq, late_m)
    acc_kl[...] = mm(sg_l[...], q_s[hq : 2 * hq], NN)
    acc_vl[...] = mm(pr_l[...], do_s[hq : 2 * hq], NN)

    ret_copy = remote(ret_send, ret_recv, ret_sems.at[0], ret_sems.at[1], in_ctx(nc - 1))

    @pl.when(is_shifted)
    def _():
        ret_send[0:half] = acc_kl[0:half].astype(BF16)
        ret_send[half:rows] = acc_vl[0:half].astype(BF16)
        ret_copy.start()

    wide = group * 128 // 2

    def send_over_dp(total, recv, sems):
        recv[here_d] = jnp.concatenate([total[:, :wide], total[:, wide:]], axis=0).astype(BF16)
        for peer in dp_peers():
            remote(recv.at[here_d], recv.at[here_d], sems.at[0], sems.at[1], peer).start()

    def send_over_ctx(recv, sems, onward, onward_sems):
        many(recv, nd - 1, sems.at[1]).wait()
        onward[here_c] = jnp.sum(recv[...].astype(F32), axis=0).astype(BF16)
        later = sorted(range(nc - 1, nc // 2 - 1, -1), key=lambda to: min(nc - to, to - nc // 2 + 1))
        for to in list(range(nc // 2)) + later:
            @pl.when(here_c != to)
            def _():
                remote(
                    onward.at[here_c], onward.at[here_c], onward_sems.at[0], onward_sems.at[1], (here_d, to, here_h)
                ).start()

    def send_halves_over_dp(total, part, recv, sems):
        for at in range(2):
            left = at * wide
            part[at] = jnp.concatenate(
                [total[:, left : left + wide // 2], total[:, left + wide // 2 : left + wide]], axis=0
            ).astype(BF16)
        recv[here_d] = part[core]
        for peer in dp_peers():
            remote(part.at[lax.rem(peer[0], 2)], recv.at[here_d], sems.at[0], sems.at[1], peer).start()

    def swap_halves(recv, sems, both, both_sems):
        many(recv, nc - 1, sems.at[1]).wait()
        both[core] = jnp.sum(recv[...].astype(F32), axis=0)
        copy = remote(
            both.at[core], both.at[core], both_sems.at[0], both_sems.at[1], (here_d + 1 - 2 * core, here_c, here_h)
        )
        copy.start()
        return copy

    def whole(recv, sems):
        many(recv, nc - 1, sems.at[1]).wait()
        total = jnp.sum(recv[...].astype(F32), axis=0)
        return jnp.concatenate([total[:rank], total[rank:]], axis=1)

    many(ri_buf, nh - 1, ri_sems.at[1]).wait()
    rank_input = jnp.sum(ri_buf[...], axis=0).astype(BF16)
    send_halves_over_dp(mm(rank_input, dqcat[...], NN) * ADAPTER_SCALE, up_p, up_a, up_asem)

    many(rg_buf, nh - 1, rg_sems.at[1]).wait()
    rank_grad = jnp.sum(rg_buf[...], axis=0).astype(BF16)
    send_over_dp(mm(rank_grad, x_s[...], NN) * ADAPTER_SCALE, dn_a, dn_asem)

    pl.semaphore_wait(relay_sems.at[1], len(two_off))
    send_over_ctx(up_a, up_asem, up_b, up_bsem)

    dkv_out[0, pl.ds(late_m, half), :] = (acc_kl[half:rows] * softmax_scale).astype(BF16)
    dkv_out[1, pl.ds(late_m, half), :] = acc_vl[half:rows].astype(BF16)

    send_over_ctx(dn_a, dn_asem, dn_b, dn_bsem)

    @pl.when(is_shifted)
    def _():
        ret_copy.wait()
        dkv_out[0, pl.ds(early_m, half), :] = (
            (acc_ke[...] + ret_recv[0:half].astype(F32)) * softmax_scale
        ).astype(BF16)
        dkv_out[1, pl.ds(early_m, half), :] = (acc_ve[...] + ret_recv[half:rows].astype(F32)).astype(BF16)

    @pl.when(jnp.logical_not(is_shifted))
    def _():
        dkv_out[0, pl.ds(early_m, half), :] = ((acc_ke[...] + acc_kl[0:half]) * softmax_scale).astype(BF16)
        dkv_out[1, pl.ds(early_m, half), :] = (acc_ve[...] + acc_vl[0:half]).astype(BF16)

    up_swap = swap_halves(up_b, up_bsem, up_c, up_csem)
    up_swap.wait()
    up_whole = jnp.concatenate(
        [up_c[at, rank * row : rank * (row + 1)] for at in range(2) for row in range(2)], axis=1
    )
    for g in range(group):
        up_out[:, g, :] = up_whole[:, g * 128 : (g + 1) * 128]
    for buf, count, sem in (
        (ri_buf, nh - 1, ri_sems), (rg_buf, nh - 1, rg_sems), (up_a, nd - 1, up_asem),
        (dn_a, nd - 1, dn_asem), (up_b, nc - 1, up_bsem), (dn_b, nc - 1, dn_bsem),
    ):
        many(buf, count, sem.at[0]).wait()
    down_out[...] = whole(dn_b, dn_bsem)


def write_out(*refs):
    dq, dkv, down, up, dq_out, dk_out, dv_out, down_out, up_out, sems = refs
    pairs = ((dq, dq_out), (dkv.at[0], dk_out), (dkv.at[1], dv_out), (down, down_out), (up, up_out))
    copies = [pltpu.make_async_copy(src, dst, sems.at[at]) for at, (src, dst) in enumerate(pairs)]
    for copy in copies:
        copy.start()
    for copy in copies:
        copy.wait()


def on_device(sizes, q, k, v, do, x, adapter_down, adapter_up, lengths):
    nd, nc, nh = sizes
    rows, group, width = q.shape[1], q.shape[3], q.shape[4]
    rank, model = adapter_down.shape[1], x.shape[2]
    half = rows // 2
    hq = half * group
    dims = (nd, nc, nh, half, group, rank)
    hbm = pl.BlockSpec(memory_space=pltpu.HBM)
    vmem = pl.BlockSpec(memory_space=pltpu.VMEM)
    pair = pltpu.SemaphoreType.DMA((2,))
    packed = (2 * rank, group * width // 2)
    halved = (2 * rank, group * width // 4)
    results = (
        ((rows * group, width), BF16),
        ((2, rows, width), BF16),
        ((rank, model), F32),
        ((rank, group, width), F32),
    )
    operands = (
        q.reshape(rows * group, width),
        k.reshape(rows, width),
        v.reshape(rows, width),
        do.reshape(rows * group, width),
        x.reshape(rows, model),
        adapter_down.T,
        adapter_up.reshape(rank * group, width),
    )
    made = pl.pallas_call(
        functools.partial(kernel, dims),
        out_shape=tuple(pltpu.VMEM(*one) for one in results),
        in_specs=[hbm] * 7 + [vmem],
        out_specs=(vmem,) * 4,
        scratch_shapes=[
            pltpu.VMEM((rows * group, width), BF16),
            pltpu.VMEM((rows * group, width), BF16),
            pltpu.VMEM((rows, model), BF16),
            pltpu.VMEM((rank, model), BF16),
            pltpu.VMEM((rank * group, width), BF16),
            pltpu.VMEM((rows + half, width), BF16),
            pltpu.VMEM((rows + half, width), BF16),
            pltpu.VMEM((rows * group, width), F32),
            pltpu.VMEM((rows, group * width), BF16),
            pltpu.VMEM((hq // CHUNK, half, CHUNK), F32),
            pltpu.VMEM((hq // CHUNK, half, CHUNK), F32),
            pltpu.VMEM((half, hq), BF16),
            pltpu.VMEM((half, hq), BF16),
            pltpu.VMEM((rows, hq), BF16),
            pltpu.VMEM((rows, hq), BF16),
            pltpu.VMEM((hq, half), BF16),
            pltpu.VMEM((half, width), F32),
            pltpu.VMEM((half, width), F32),
            pltpu.VMEM((rows, width), F32),
            pltpu.VMEM((rows, width), F32),
            pltpu.VMEM((rows, width), BF16),
            pltpu.VMEM((rows, width), BF16),
            pltpu.VMEM((nh, rank, rows), F32),
            pltpu.VMEM((nh, rank, rows), F32),
        ]
        + [
            pltpu.VMEM((2,) + halved, BF16),
            pltpu.VMEM((nd,) + halved, BF16),
            pltpu.VMEM((nc,) + halved, BF16),
            pltpu.VMEM((2,) + halved, F32),
            pltpu.VMEM((nd,) + packed, BF16),
            pltpu.VMEM((nc,) + packed, BF16),
        ]
        + [pltpu.SemaphoreType.DMA((12,))]
        + [pair] * 10
        + [pltpu.SemaphoreType.REGULAR((2,))],
        compiler_params=pltpu.CompilerParams(
            collective_id=0, has_side_effects=True, vmem_limit_bytes=40 * 1024 * 1024
        ),
        name="attention_and_rank_gradients",
    )(
        *(pltpu.with_memory_space_constraint(one, pltpu.HBM) for one in operands),
        pltpu.with_memory_space_constraint(jnp.broadcast_to(lengths[:, None], (1, CHUNK)), pltpu.VMEM),
    )
    dq, dk, dv, down, up = pl.pallas_call(
        write_out,
        out_shape=(
            jax.ShapeDtypeStruct(*results[0]),
            jax.ShapeDtypeStruct((rows, width), BF16),
            jax.ShapeDtypeStruct((rows, width), BF16),
            jax.ShapeDtypeStruct(*results[2]),
            jax.ShapeDtypeStruct(*results[3]),
        ),
        in_specs=[vmem] * 4,
        out_specs=(hbm,) * 5,
        scratch_shapes=[pltpu.SemaphoreType.DMA((5,))],
        name="write_results",
    )(*(pltpu.with_memory_space_constraint(one, pltpu.VMEM) for one in made))
    return (
        dq.reshape(q.shape),
        dk.reshape(k.shape),
        dv.reshape(v.shape),
        down.T,
        up.reshape(adapter_up.shape),
    )


def solution(mesh):
    sizes = (mesh.shape["dp"], mesh.shape["ctx"], mesh.shape["head"])
    return jax.shard_map(
        functools.partial(on_device, sizes),
        mesh=mesh,
        in_specs=(
            P("dp", "ctx", "head", None, None),
            P("dp", "ctx", "head", None),
            P("dp", "ctx", "head", None),
            P("dp", "ctx", "head", None, None),
            P("dp", "ctx", "head"),
            P("head", None),
            P(None, "head", None, None),
            P("dp"),
        ),
        out_specs=(
            P("dp", "ctx", "head", None, None),
            P("dp", "ctx", "head", None),
            P("dp", "ctx", "head", None),
            P("head", None),
            P(None, "head", None, None),
        ),
        check_vma=False,
    )
```

```python
import functools
import math

import jax
import jax.numpy as jnp
from jax import lax
from jax.experimental import pallas as pl
from jax.experimental.pallas import tpu as pltpu
from jax.sharding import PartitionSpec as P

ADAPTER_SCALE = 2.0
BLOCKED = -1e30
CHUNK = 512
MESH = pl.DeviceIdType.MESH
F32 = jnp.float32
BF16 = jnp.bfloat16
NT = (((1,), (1,)), ((), ()))
NN = (((1,), (0,)), ((), ()))
TN = (((0,), (0,)), ((), ()))


def far_first(count):
    return sorted(range(1, count), key=lambda step: -min(step, count - step))


def mm(a, b, dims):
    return lax.dot_general(a, b, dims, preferred_element_type=F32)


def kernel(
    dims,
    q_in, k_in, v_in, do_in, x_in, at_in, u_in, len_in,
    dq_out, dkv_out, down_out, up_out,
    q_s, do_s, x_s, at_s, u_s, k_s, v_s,
    dq32, dqcat, own_scores, own_grads, sg_e, pr_e, sg_l, pr_l,
    acc_ke, acc_ve, acc_kl, acc_vl, ret_send, ret_recv,
    ri_buf, rg_buf, up_p, up_a, up_b, up_c, dn_a, dn_b,
    load_sem, kv_send, kv_recv, ret_sems, ri_sems, rg_sems,
    up_asem, up_bsem, up_csem, dn_asem, dn_bsem, relay_sems,
):
    nd, nc, nh, half, group, rank = dims
    rows = 2 * half
    hq = half * group
    here_d, here_c, here_h = lax.axis_index("dp"), lax.axis_index("ctx"), lax.axis_index("head")
    is_shifted = here_h < nh // 2
    core = lax.rem(here_d, 2)
    shifted = jnp.where(is_shifted, 1, 0)
    early = shifted * half
    late = (1 - shifted) * half
    early_q = pl.multiple_of(shifted * hq, hq)
    late_q = pl.multiple_of((1 - shifted) * hq, hq)
    early_m = pl.multiple_of(early, half)
    late_m = pl.multiple_of(late, half)
    after_c = lax.rem(here_c + 1, nc)
    before_c = lax.rem(here_c + nc - 1, nc)

    def in_head(step):
        return (here_d, here_c, lax.rem(here_h + step, nh))

    def in_ctx(step):
        return (here_d, lax.rem(here_c + step, nc), here_h)

    def dp_peers():
        moves = [(x, c) for x in range(nd // 2 - 1, -1, -1) for c in (1, 0) if (x, c) != (0, 0)]
        return [
            (lax.rem(here_d // 2 + x, nd // 2) * 2 + lax.rem(core + c, 2), here_c, here_h) for x, c in moves
        ]

    def head_peers():
        ny, side = nh // 2, lax.rem(here_h, 2)
        moves = [(y, x) for y in range(ny) for x in range(2) if (y, x) != (0, 0)]
        moves.sort(key=lambda move: -(min(move[0], ny - move[0]) + 2 * move[1]))
        return [
            (here_d, here_c, lax.rem(here_h // 2 + y, ny) * 2 + lax.rem(side + x, 2)) for y, x in moves
        ]

    flip = (here_d, here_c, here_h + 1 - 2 * lax.rem(here_h, 2))
    beside = [in_ctx(step) for step in sorted({1, nc - 1})]
    two_off = [in_ctx(step) for step in sorted({2, nc - 2}) if 0 < step < nc]
    near = (
        [flip]
        + [in_head(step) for step in sorted({2, 4, nh - 2}) if 0 < step < nh]
        + dp_peers()
        + beside
    )

    def tell(semaphore, peers):
        for peer in peers:
            pl.semaphore_signal(semaphore, inc=1, device_id=peer, device_id_type=MESH)

    barrier = pltpu.get_barrier_semaphore()
    tell(barrier, near)

    def local(src, dst, at):
        copy = pltpu.make_async_copy(src, dst, load_sem.at[at])
        copy.start()
        return copy

    load_ke = local(k_in.at[pl.ds(early_m, half)], k_s.at[pl.ds(0, half)], 0)
    load_ve = local(v_in.at[pl.ds(early_m, half)], v_s.at[pl.ds(0, half)], 1)
    load_qe = local(q_in.at[pl.ds(early_q, hq)], q_s.at[pl.ds(0, hq)], 2)
    load_de = local(do_in.at[pl.ds(early_q, hq)], do_s.at[pl.ds(0, hq)], 3)
    load_x = local(x_in, x_s, 5)
    load_at = local(at_in, at_s, 6)
    load_kl = local(k_in.at[pl.ds(late_m, half)], k_s.at[pl.ds(rows, half)], 7)
    load_vl = local(v_in.at[pl.ds(late_m, half)], v_s.at[pl.ds(rows, half)], 8)
    load_ql = local(q_in.at[pl.ds(late_q, hq)], q_s.at[pl.ds(hq, hq)], 9)
    load_dl = local(do_in.at[pl.ds(late_q, hq)], do_s.at[pl.ds(hq, hq)], 10)
    load_u = local(u_in, u_s, 11)

    def remote(src, dst, sends, recvs, peer):
        return pltpu.make_async_remote_copy(
            src_ref=src, dst_ref=dst, send_sem=sends, recv_sem=recvs, device_id=peer, device_id_type=MESH
        )

    def many(buf, count, sem):
        part = buf.at[pl.ds(0, count)]
        return pltpu.make_async_copy(part, part, sem)

    softmax_scale = 1.0 / math.sqrt(128)
    exp_scale = softmax_scale * math.log2(math.e)
    chunk = CHUNK
    per = chunk // group
    chunks = hq // chunk
    start_early = here_c * rows + early
    start_late = here_c * rows + late
    start_prev = jnp.where(is_shifted, before_c * rows + half, start_early)
    load_ke.wait()
    load_ve.wait()
    length = len_in[...]

    def own_part(at, keys, values, queries, live, base):
        key_at = lax.broadcasted_iota(jnp.int32, (half, chunk), 0)
        query_at = lax.broadcasted_iota(jnp.int32, (half, chunk), 1) // group + at * per
        allowed = (key_at <= query_at) & ((key_at < length - base) | (key_at == query_at))
        scores = jnp.where(allowed, mm(keys, queries, NT), BLOCKED)
        return scores, mm(values, live, NT)

    def finish(at, scores, prob_grad, keys, base, to, row0, grads_to, probs_to):
        top = jnp.max(scores, axis=0, keepdims=True)
        weights = jnp.exp2((scores - top) * exp_scale)
        total = jnp.sum(weights, axis=0, keepdims=True)
        query_row = lax.broadcasted_iota(jnp.int32, (1, chunk), 1) // group + at * per
        inverse = jnp.where(query_row < length - base, 1.0 / total, 0.0)
        probs = weights * inverse
        probs_low = probs.astype(BF16)
        out_dot = jnp.sum(probs_low.astype(F32) * prob_grad, axis=0, keepdims=True)
        score_grad = (probs * (prob_grad - out_dot)).astype(BF16)
        query_grad = mm(score_grad, keys, TN) * softmax_scale
        dq32[row0 + at * chunk : row0 + (at + 1) * chunk] = query_grad
        dq_out[pl.ds(pl.multiple_of(to + at * chunk, chunk), chunk), :] = query_grad.astype(BF16)
        lanes = slice(at * chunk, (at + 1) * chunk)
        grads_to[:, lanes] = score_grad
        probs_to[:, lanes] = probs_low

    def rank_part(row0, to):
        for g in range(group):
            dqcat[pl.ds(to, half), g * 128 : (g + 1) * 128] = dq32[pl.ds(row0 + g, half, stride=group), :].astype(
                BF16
            )
        rg_buf[here_h, :, pl.ds(to, half)] = mm(up_flat, dqcat[pl.ds(to, half), :], NT)

    pl.semaphore_wait(barrier, len(near))
    kv_copies = [
        remote(ref.at[pl.ds(0, half)], ref.at[pl.ds(half, half)], kv_send.at[at], kv_recv.at[at], in_ctx(1))
        for at, ref in enumerate((k_s, v_s))
    ]

    @pl.when(is_shifted)
    def _():
        for copy in kv_copies:
            copy.start()

    @pl.when(jnp.logical_not(is_shifted))
    def _():
        k_s[half:rows] = k_s[0:half]
        v_s[half:rows] = v_s[0:half]

    tell(relay_sems.at[0], [flip] + beside)

    load_qe.wait()
    load_de.wait()
    for at in range(chunks):
        place = slice(at * chunk, (at + 1) * chunk)
        keys = k_s[0:half]
        scores, prob_grad = own_part(at, keys, v_s[0:half], q_s[place], do_s[place], start_early)
        finish(at, scores, prob_grad, keys, start_early, early_q, 0, sg_e, pr_e)

    def head_exchange(buf, sems):
        for peer in head_peers():
            remote(buf.at[here_h], buf.at[here_h], sems.at[0], sems.at[1], peer).start()

    load_x.wait()
    load_at.wait()
    ri_buf[here_h] = mm(at_s[...], x_s[...], NT)
    load_kl.wait()
    load_vl.wait()
    load_ql.wait()
    load_dl.wait()
    for at in range(chunks):
        place = slice(hq + at * chunk, hq + (at + 1) * chunk)
        scores, prob_grad = own_part(
            at, k_s[rows : rows + half], v_s[rows : rows + half], q_s[place], do_s[place], start_late
        )
        own_scores[at] = scores
        own_grads[at] = prob_grad
    load_u.wait()
    up_flat = jnp.concatenate(
        [u_s[...].astype(F32).reshape(rank, group, 128)[:, g, :] for g in range(group)], axis=1
    ).astype(BF16)
    rank_part(0, early_m)
    acc_ke[...] = mm(sg_e[...], q_s[0:hq], NN)
    acc_ve[...] = mm(pr_e[...], do_s[0:hq], NN)
    pl.semaphore_wait(relay_sems.at[0], 1 + len(beside))
    head_exchange(ri_buf, ri_sems)
    tell(relay_sems.at[1], two_off)


    @pl.when(is_shifted)
    def _():
        for copy in kv_copies:
            copy.wait()

    prev_seen = lax.broadcasted_iota(jnp.int32, (half, chunk), 0) < length - start_prev
    for at in range(chunks):
        place = slice(hq + at * chunk, hq + (at + 1) * chunk)
        prev_scores = jnp.where(prev_seen, mm(k_s[half:rows], q_s[place], NT), BLOCKED)
        scores = jnp.concatenate([prev_scores, own_scores[at]], axis=0)
        prob_grad = jnp.concatenate([mm(v_s[half:rows], do_s[place], NT), own_grads[at]], axis=0)
        finish(at, scores, prob_grad, k_s[half : rows + half], start_late, late_q, hq, sg_l, pr_l)

    rank_part(hq, late_m)
    head_exchange(rg_buf, rg_sems)
    acc_kl[...] = mm(sg_l[...], q_s[hq : 2 * hq], NN)
    acc_vl[...] = mm(pr_l[...], do_s[hq : 2 * hq], NN)

    ret_copy = remote(ret_send, ret_recv, ret_sems.at[0], ret_sems.at[1], in_ctx(nc - 1))

    @pl.when(is_shifted)
    def _():
        ret_send[0:half] = acc_kl[0:half].astype(BF16)
        ret_send[half:rows] = acc_vl[0:half].astype(BF16)
        ret_copy.start()

    wide = group * 128 // 2

    def send_over_dp(total, recv, sems):
        recv[here_d] = jnp.concatenate([total[:, :wide], total[:, wide:]], axis=0).astype(BF16)
        for peer in dp_peers():
            remote(recv.at[here_d], recv.at[here_d], sems.at[0], sems.at[1], peer).start()

    def send_over_ctx(recv, sems, onward, onward_sems):
        many(recv, nd - 1, sems.at[1]).wait()
        onward[here_c] = jnp.sum(recv[...].astype(F32), axis=0).astype(BF16)
        later = sorted(range(nc - 1, nc // 2 - 1, -1), key=lambda to: min(nc - to, to - nc // 2 + 1))
        for to in list(range(nc // 2)) + later:
            @pl.when(here_c != to)
            def _():
                remote(
                    onward.at[here_c], onward.at[here_c], onward_sems.at[0], onward_sems.at[1], (here_d, to, here_h)
                ).start()

    def send_halves_over_dp(total, part, recv, sems):
        for at in range(2):
            left = at * wide
            part[at] = jnp.concatenate(
                [total[:, left : left + wide // 2], total[:, left + wide // 2 : left + wide]], axis=0
            ).astype(BF16)
        recv[here_d] = part[core]
        for peer in dp_peers():
            remote(part.at[lax.rem(peer[0], 2)], recv.at[here_d], sems.at[0], sems.at[1], peer).start()

    def swap_halves(recv, sems, both, both_sems):
        many(recv, nc - 1, sems.at[1]).wait()
        both[core] = jnp.sum(recv[...].astype(F32), axis=0)
        copy = remote(
            both.at[core], both.at[core], both_sems.at[0], both_sems.at[1], (here_d + 1 - 2 * core, here_c, here_h)
        )
        copy.start()
        return copy

    def whole(recv, sems):
        many(recv, nc - 1, sems.at[1]).wait()
        total = jnp.sum(recv[...].astype(F32), axis=0)
        return jnp.concatenate([total[:rank], total[rank:]], axis=1)

    many(ri_buf, nh - 1, ri_sems.at[1]).wait()
    rank_input = jnp.sum(ri_buf[...], axis=0).astype(BF16)
    send_halves_over_dp(mm(rank_input, dqcat[...], NN) * ADAPTER_SCALE, up_p, up_a, up_asem)

    many(rg_buf, nh - 1, rg_sems.at[1]).wait()
    rank_grad = jnp.sum(rg_buf[...], axis=0).astype(BF16)
    send_over_dp(mm(rank_grad, x_s[...], NN) * ADAPTER_SCALE, dn_a, dn_asem)

    pl.semaphore_wait(relay_sems.at[1], len(two_off))
    send_over_ctx(up_a, up_asem, up_b, up_bsem)

    dkv_out[0, pl.ds(late_m, half), :] = (acc_kl[half:rows] * softmax_scale).astype(BF16)
    dkv_out[1, pl.ds(late_m, half), :] = acc_vl[half:rows].astype(BF16)

    send_over_ctx(dn_a, dn_asem, dn_b, dn_bsem)

    @pl.when(is_shifted)
    def _():
        ret_copy.wait()
        dkv_out[0, pl.ds(early_m, half), :] = (
            (acc_ke[...] + ret_recv[0:half].astype(F32)) * softmax_scale
        ).astype(BF16)
        dkv_out[1, pl.ds(early_m, half), :] = (acc_ve[...] + ret_recv[half:rows].astype(F32)).astype(BF16)

    @pl.when(jnp.logical_not(is_shifted))
    def _():
        dkv_out[0, pl.ds(early_m, half), :] = ((acc_ke[...] + acc_kl[0:half]) * softmax_scale).astype(BF16)
        dkv_out[1, pl.ds(early_m, half), :] = (acc_ve[...] + acc_vl[0:half]).astype(BF16)

    up_swap = swap_halves(up_b, up_bsem, up_c, up_csem)
    up_swap.wait()
    up_whole = jnp.concatenate(
        [up_c[at, rank * row : rank * (row + 1)] for at in range(2) for row in range(2)], axis=1
    )
    for g in range(group):
        up_out[:, g, :] = up_whole[:, g * 128 : (g + 1) * 128]
    for buf, count, sem in (
        (ri_buf, nh - 1, ri_sems), (rg_buf, nh - 1, rg_sems), (up_a, nd - 1, up_asem),
        (dn_a, nd - 1, dn_asem), (up_b, nc - 1, up_bsem), (dn_b, nc - 1, dn_bsem),
    ):
        many(buf, count, sem.at[0]).wait()
    down_out[...] = whole(dn_b, dn_bsem)


def write_out(*refs):
    dq, dkv, down, up, dq_out, dk_out, dv_out, down_out, up_out, sems = refs
    pairs = ((dq, dq_out), (dkv.at[0], dk_out), (dkv.at[1], dv_out), (down, down_out), (up, up_out))
    copies = [pltpu.make_async_copy(src, dst, sems.at[at]) for at, (src, dst) in enumerate(pairs)]
    for copy in copies:
        copy.start()
    for copy in copies:
        copy.wait()


def on_device(sizes, q, k, v, do, x, adapter_down, adapter_up, lengths):
    nd, nc, nh = sizes
    rows, group, width = q.shape[1], q.shape[3], q.shape[4]
    rank, model = adapter_down.shape[1], x.shape[2]
    half = rows // 2
    hq = half * group
    dims = (nd, nc, nh, half, group, rank)
    hbm = pl.BlockSpec(memory_space=pltpu.HBM)
    vmem = pl.BlockSpec(memory_space=pltpu.VMEM)
    pair = pltpu.SemaphoreType.DMA((2,))
    packed = (2 * rank, group * width // 2)
    halved = (2 * rank, group * width // 4)
    results = (
        ((rows * group, width), BF16),
        ((2, rows, width), BF16),
        ((rank, model), F32),
        ((rank, group, width), F32),
    )
    operands = (
        q.reshape(rows * group, width),
        k.reshape(rows, width),
        v.reshape(rows, width),
        do.reshape(rows * group, width),
        x.reshape(rows, model),
        adapter_down.T,
        adapter_up.reshape(rank * group, width),
    )
    made = pl.pallas_call(
        functools.partial(kernel, dims),
        out_shape=tuple(pltpu.VMEM(*one) for one in results),
        in_specs=[hbm] * 7 + [vmem],
        out_specs=(vmem,) * 4,
        scratch_shapes=[
            pltpu.VMEM((rows * group, width), BF16),
            pltpu.VMEM((rows * group, width), BF16),
            pltpu.VMEM((rows, model), BF16),
            pltpu.VMEM((rank, model), BF16),
            pltpu.VMEM((rank * group, width), BF16),
            pltpu.VMEM((rows + half, width), BF16),
            pltpu.VMEM((rows + half, width), BF16),
            pltpu.VMEM((rows * group, width), F32),
            pltpu.VMEM((rows, group * width), BF16),
            pltpu.VMEM((hq // CHUNK, half, CHUNK), F32),
            pltpu.VMEM((hq // CHUNK, half, CHUNK), F32),
            pltpu.VMEM((half, hq), BF16),
            pltpu.VMEM((half, hq), BF16),
            pltpu.VMEM((rows, hq), BF16),
            pltpu.VMEM((rows, hq), BF16),
            pltpu.VMEM((half, width), F32),
            pltpu.VMEM((half, width), F32),
            pltpu.VMEM((rows, width), F32),
            pltpu.VMEM((rows, width), F32),
            pltpu.VMEM((rows, width), BF16),
            pltpu.VMEM((rows, width), BF16),
            pltpu.VMEM((nh, rank, rows), F32),
            pltpu.VMEM((nh, rank, rows), F32),
        ]
        + [
            pltpu.VMEM((2,) + halved, BF16),
            pltpu.VMEM((nd,) + halved, BF16),
            pltpu.VMEM((nc,) + halved, BF16),
            pltpu.VMEM((2,) + halved, F32),
            pltpu.VMEM((nd,) + packed, BF16),
            pltpu.VMEM((nc,) + packed, BF16),
        ]
        + [pltpu.SemaphoreType.DMA((12,))]
        + [pair] * 10
        + [pltpu.SemaphoreType.REGULAR((2,))],
        compiler_params=pltpu.CompilerParams(
            collective_id=0, has_side_effects=True, vmem_limit_bytes=40 * 1024 * 1024
        ),
        name="attention_and_rank_gradients",
    )(
        *(pltpu.with_memory_space_constraint(one, pltpu.HBM) for one in operands),
        pltpu.with_memory_space_constraint(jnp.broadcast_to(lengths[:, None], (1, CHUNK)), pltpu.VMEM),
    )
    dq, dk, dv, down, up = pl.pallas_call(
        write_out,
        out_shape=(
            jax.ShapeDtypeStruct(*results[0]),
            jax.ShapeDtypeStruct((rows, width), BF16),
            jax.ShapeDtypeStruct((rows, width), BF16),
            jax.ShapeDtypeStruct(*results[2]),
            jax.ShapeDtypeStruct(*results[3]),
        ),
        in_specs=[vmem] * 4,
        out_specs=(hbm,) * 5,
        scratch_shapes=[pltpu.SemaphoreType.DMA((5,))],
        name="write_results",
    )(*(pltpu.with_memory_space_constraint(one, pltpu.VMEM) for one in made))
    return (
        dq.reshape(q.shape),
        dk.reshape(k.shape),
        dv.reshape(v.shape),
        down.T,
        up.reshape(adapter_up.shape),
    )


def solution(mesh):
    sizes = (mesh.shape["dp"], mesh.shape["ctx"], mesh.shape["head"])
    return jax.shard_map(
        functools.partial(on_device, sizes),
        mesh=mesh,
        in_specs=(
            P("dp", "ctx", "head", None, None),
            P("dp", "ctx", "head", None),
            P("dp", "ctx", "head", None),
            P("dp", "ctx", "head", None, None),
            P("dp", "ctx", "head"),
            P("head", None),
            P(None, "head", None, None),
            P("dp"),
        ),
        out_specs=(
            P("dp", "ctx", "head", None, None),
            P("dp", "ctx", "head", None),
            P("dp", "ctx", "head", None),
            P("head", None),
            P(None, "head", None, None),
        ),
        check_vma=False,
    )
```
